128 devices in a mesh: kv: 16 (over x, z), tp: 8 (over y, core).
Axes of the slice: x: 4, y: 4, z: 4, core: 2. Of those that a mesh axis runs over, the one named last changes fastest.
Arguments:
- queries: bfloat16 [16, 16384], P('kv', 'tp'), may hold values from -16 to 16
- sign_bits: int32 [128], replicated, may hold values from 0 to 1
- key_pages: bfloat16 [512, 256, 1024], P('kv', None, 'tp'), may hold values from -16 to 16
- value_pages: bfloat16 [512, 256, 1024], P('kv', None, 'tp'), may hold values from -6 to 6
- page_table: int32 [16, 16, 4], P('kv'), may hold values from 0 to 31, as said below
- page_count: int32 [16, 16], P('kv'), may hold values from 0 to 4, as said below
- residual: bfloat16 [16, 16384], P(None, 'tp'), may hold values from -8 to 8
- norm_gain: bfloat16 [16384], P('tp'), may hold values from 0.099609375 to 1.8984375
- gate_weight: bfloat16 [16384, 26624], P('tp', 'kv'), may hold values from -0.046875 to 0.046875
- up_weight: bfloat16 [16384, 26624], P('tp', 'kv'), may hold values from -0.046875 to 0.046875
- down_weight: bfloat16 [26624, 16384], P('kv', 'tp'), may hold values from -0.0390625 to 0.0390625
Outputs:
- layer_out: bfloat16 [16, 16384], P('kv', 'tp')
The draws below stay inside these ranges and needn't reach their ends.
Inputs may be any that keep to these rules, and one draw needn't show every extreme that they name: `page_count`: on each device one request holds exactly 4 pages; every request owns at least one page on some device; a device's live pages number at most 32 and some pool pages may be owned by nobody. `page_table`: live entries of one device are distinct pool pages; entries past a list's count are arbitrary pool pages.
All inputs are finite; a program needn't handle non-finite values.
Results may differ from the reference program's by a relative error of at most 0.019.
Values may be sent and summed in bfloat16 or wider, within the bound.
A program may use at most 128 MiB of HBM per device.

```python
import jax
import jax.numpy as jnp
from jax import lax

HEADS = 128
KVH = 8
HD = 128
D = 16384
FF = 26624
PAGE = 256
MAXP = 4
PAGES_DEV = 32
REQS = 16
ALL_PAGES = 512


def layout(key):
    spare = PAGES_DEV - MAXP
    shards = ALL_PAGES // PAGES_DEV
    order = jax.random.permutation(jax.random.fold_in(key, 101), REQS).astype(jnp.int32)
    shard_ids = jnp.arange(shards, dtype=jnp.int32)
    places = (shard_ids[:, None] * spare + jnp.arange(spare, dtype=jnp.int32)[None, :]) % REQS
    window = order[places]
    counts = jnp.sum((window[:, :, None] == jnp.arange(REQS, dtype=jnp.int32)[None, None, :]).astype(jnp.int32), axis=1)
    heavy = order[(shard_ids * spare + spare) % REQS]
    is_heavy = jnp.arange(REQS, dtype=jnp.int32)[None, :] == heavy[:, None]
    counts = jnp.where(is_heavy, MAXP, counts).astype(jnp.int32)
    starts = jnp.cumsum(counts, axis=1) - counts

    def one_shard(shard, start_row, count_row):
        shard_key = jax.random.fold_in(jax.random.fold_in(key, 202), shard)
        shuffled = jax.random.permutation(shard_key, PAGES_DEV).astype(jnp.int32)
        slots = jnp.arange(MAXP, dtype=jnp.int32)[None, :]
        where_at = jnp.minimum(start_row[:, None] + slots, PAGES_DEV - 1)
        padding = jax.random.randint(jax.random.fold_in(shard_key, 1), (REQS, MAXP), 0, PAGES_DEV, dtype=jnp.int32)
        return jnp.where(slots < count_row[:, None], shuffled[where_at], padding)
    table = jax.vmap(one_shard)(shard_ids, starts, counts)
    return (table, counts)


def planting(key):
    signs = jax.random.randint(jax.random.fold_in(key, 31), (HD,), 0, 2, dtype=jnp.int32)
    return signs


def draw_page_table(key, part):
    return layout(key)[0]


def draw_page_count(key, part):
    return layout(key)[1]


def draw_sign_bits(key, part):
    return planting(key)


def draw_queries(key, part):
    key = jax.random.fold_in(key, 41)
    base = jax.random.normal(key, (REQS, HEADS, HD), jnp.float32)
    return jnp.clip(base, -16.0, 16.0).reshape(REQS, HEADS * HD).astype(jnp.bfloat16)


def draw_key_pages(key, part):
    key = jax.random.fold_in(key, 43)
    base = jnp.clip(2.5 * jax.random.normal(key, (ALL_PAGES, PAGE, KVH, HD), jnp.float32), -16.0, 16.0)
    return base.reshape(ALL_PAGES, PAGE, KVH * HD).astype(jnp.bfloat16)


def draw_residual(key, part):
    key = jax.random.fold_in(key, 47)
    position = jnp.arange(D, dtype=jnp.float32)[None, :] / D
    base = jax.random.normal(key, (REQS, D), jnp.float32) * (0.1 * jnp.exp(2.302585 * position))
    return jnp.clip(base, -8.0, 8.0).astype(jnp.bfloat16)


def level_of(key, dims, cuts, smallest, high):
    level = 1.0
    for dim, shards_of in cuts:
        draws = jax.random.uniform(jax.random.fold_in(jax.random.fold_in(key, 6), dim), (shards_of,), jnp.float32, smallest / len(cuts), high / len(cuts))
        level = level * jnp.repeat(jnp.exp(draws), dims[dim] // shards_of).reshape((-1,) + (1,) * (len(dims) - 1 - dim))
    return level


def centred(rng, dims, width, limit, cuts=(), held_as=jnp.bfloat16):
    result = jax.random.normal(rng, dims, jnp.float32) * width
    if len(cuts) > 0:
        result = level_of(rng, dims, cuts, -0.22, 0.18) * result
    return jnp.clip(result, min=-limit, max=limit).astype(held_as)


def setup_inputs(seed: int = 0) -> dict:
    arg_keys = jax.random.split(jax.random.key(seed), 12)
    queries = draw_queries(jax.random.fold_in(arg_keys[11], 71), 0)
    sign_bits = draw_sign_bits(jax.random.fold_in(arg_keys[11], 71), 0)
    key_pages = draw_key_pages(jax.random.fold_in(arg_keys[11], 71), 0)
    value_pages = centred(arg_keys[3], (ALL_PAGES, PAGE, KVH * HD), 1.0, 6.0, ((0, 16), (2, 8)))
    page_table = draw_page_table(jax.random.fold_in(arg_keys[11], 71), 0)
    page_count = draw_page_count(jax.random.fold_in(arg_keys[11], 71), 0)
    residual = draw_residual(jax.random.fold_in(arg_keys[11], 71), 0)
    norm_gain = jnp.clip(1.0 + 0.18 * jax.random.normal(arg_keys[7], (D,), jnp.float32), 0.099609375, 1.8984375).astype(jnp.bfloat16)
    gate_weight = centred(arg_keys[8], (D, FF), D ** -0.5, 0.046875, ((0, 8), (1, 16)))
    up_weight = centred(arg_keys[9], (D, FF), D ** -0.5, 0.046875, ((0, 8), (1, 16)))
    down_weight = centred(arg_keys[10], (FF, D), FF ** -0.5, 0.0390625, ((0, 16), (1, 8)))
    return {"queries": queries, "sign_bits": sign_bits, "key_pages": key_pages, "value_pages": value_pages, "page_table": page_table, "page_count": page_count, "residual": residual, "norm_gain": norm_gain, "gate_weight": gate_weight, "up_weight": up_weight, "down_weight": down_weight}


fill_value = -1e+30
epsilon = 1e-05

def sylvester(size):
    index = jnp.arange(size, dtype=jnp.int32)
    common = jnp.bitwise_and(index[:, None], index[None, :])
    parity = jnp.zeros((size, size), jnp.int32)
    for level in range(size.bit_length() - 1):
        parity = parity + jnp.bitwise_and(jnp.right_shift(common, level), 1)
    return (1 - 2 * (parity % 2)).astype(jnp.float32)

def reference(queries, sign_bits, key_pages, value_pages, page_table, page_count, residual, norm_gain, gate_weight, up_weight, down_weight):
    highest = lax.Precision.HIGHEST
    signs = (1 - 2 * sign_bits).astype(jnp.float32)
    signed = queries.astype(jnp.float32).reshape(REQS, HEADS, HD) * signs
    rotated = (jnp.einsum('rhd,de->rhe', signed, sylvester(HD), precision=highest) / HD).astype(jnp.bfloat16)
    shards = ALL_PAGES // PAGES_DEV
    live = jnp.arange(MAXP, dtype=jnp.int32)[None, None, :] < page_count[:, :, None]
    match = (page_table[:, :, :, None] == jnp.arange(PAGES_DEV, dtype=jnp.int32)[None, None, None, :]) & live[:, :, :, None]
    owned = lax.optimization_barrier(jnp.sum(match.astype(jnp.float32), axis=2))
    owned = owned.transpose(1, 0, 2).reshape(REQS, shards * PAGES_DEV)
    per_group = HEADS // KVH
    grouped = rotated.reshape(REQS, KVH, per_group, HD).transpose(1, 0, 2, 3)
    keys = key_pages.reshape(ALL_PAGES, PAGE, KVH, HD).transpose(2, 0, 1, 3)
    values = value_pages.reshape(ALL_PAGES, PAGE, KVH, HD).transpose(2, 0, 1, 3)

    def one_group(items):
        query_group, key_group, value_group = items
        page_queries = jnp.einsum('rp,rqd->pqd', owned, query_group.astype(jnp.float32), precision=highest)
        scores = jnp.einsum('pqd,ptd->pqt', page_queries, key_group.astype(jnp.float32), precision=highest)
        page_max = lax.optimization_barrier(jnp.max(scores, axis=-1))
        weights = jnp.exp(scores - page_max[..., None]).astype(jnp.bfloat16).astype(jnp.float32)
        page_total = lax.optimization_barrier(jnp.sum(weights, axis=-1))
        page_out = jnp.einsum('pqt,ptd->pqd', weights, value_group.astype(jnp.float32), precision=highest)
        mask = (owned > 0)[:, :, None]
        masked = jnp.where(mask, page_max[None], fill_value)
        best = lax.optimization_barrier(jnp.max(masked, axis=1))
        factor = jnp.where(mask, jnp.exp(masked - best[:, None]), 0.0)
        total = jnp.einsum('rpq,pq->rq', factor, page_total, precision=highest)
        merged = jnp.einsum('rpq,pqd->rqd', factor, page_out, precision=highest)
        return (merged / total[..., None]).astype(jnp.bfloat16)
    attention = lax.map(one_group, (grouped, keys, values))
    attention = attention.transpose(1, 0, 2, 3).reshape(REQS, HEADS * HD)
    stream = residual.astype(jnp.float32) + attention.astype(jnp.float32)
    inverse = lax.rsqrt(lax.optimization_barrier(jnp.mean(stream * stream, axis=-1)) + epsilon)[:, None]
    scaled = (stream * norm_gain.astype(jnp.float32)).astype(jnp.bfloat16)
    gate = jnp.dot(scaled, gate_weight, preferred_element_type=jnp.float32) * inverse
    upper = jnp.dot(scaled, up_weight, preferred_element_type=jnp.float32) * inverse
    hidden = (jax.nn.silu(gate) * upper).astype(jnp.bfloat16)
    return (stream + jnp.dot(hidden, down_weight, preferred_element_type=jnp.float32)).astype(jnp.bfloat16)
```

```python
from functools import partial

import jax
import jax.numpy as jnp
from jax import lax
from jax.experimental import pallas as pl
from jax.experimental.pallas import tpu as pltpu
from jax.sharding import PartitionSpec as P

fill_value = -1e30
epsilon = 1e-05
f32 = jnp.float32
bf16 = jnp.bfloat16
MESH = pl.DeviceIdType.MESH

KV = 16
TP = 8
HEADS = 16
HD = 128
SLOTS = 4
FEATURES = HEADS * HD
UNITS = 1664
CHUNK = 256
WHOLE = UNITS // CHUNK
TAIL = UNITS - WHOLE * CHUNK
CHUNKS = WHOLE + 1


def dot(left, right):
    return jnp.dot(left, right, preferred_element_type=f32)


def split3(value):
    high = value.astype(bf16).astype(f32)
    rest = value - high
    middle = rest.astype(bf16).astype(f32)
    return high, middle, rest - middle


def in_lanes(parts):
    rows = parts[0].shape[0]
    lane = lax.broadcasted_iota(jnp.int32, (rows, 128), 1)
    tile = jnp.zeros((rows, 128), f32)
    for place, part in enumerate(parts):
        tile = jnp.where(lane == place, part, tile)
    return tile.astype(bf16)


def layer(
    table,
    count,
    queries_hbm,
    signs_hbm,
    keys_hbm,
    values_hbm,
    residual_hbm,
    gain_hbm,
    gate_hbm,
    up_hbm,
    down_hbm,
    out,
    queries,
    signs,
    keys,
    values,
    residual,
    gain,
    gate,
    up,
    down,
    rotated,
    part_out,
    part_in,
    attended,
    stage,
    scaled,
    square_out,
    square_in,
    sums_out,
    sums_in,
    hidden,
    mixed_out,
    mixed_in,
    load_sem,
    send_sem,
    recv_sem,
):
    kv = lax.axis_index("kv")
    tp = lax.axis_index("tp")

    loads = [
        pltpu.make_async_copy(source, target, load_sem.at[place])
        for place, (source, target) in enumerate(
            [
                (queries_hbm, queries),
                (signs_hbm, signs),
                (residual_hbm, residual),
                (gain_hbm, gain),
                (keys_hbm, keys),
                (values_hbm, values),
                (gate_hbm, gate),
                (up_hbm, up),
                (down_hbm, down),
            ]
        )
    ]
    for load in loads:
        load.start()

    barrier = pltpu.get_barrier_semaphore()

    def greet_kv(step, carry):
        pl.semaphore_signal(
            barrier, inc=1, device_id={"kv": lax.rem(kv + step, KV)}, device_id_type=MESH
        )
        return carry

    def greet_tp(step, carry):
        pl.semaphore_signal(
            barrier, inc=1, device_id={"tp": lax.rem(tp + step, TP)}, device_id_type=MESH
        )
        return carry

    lax.fori_loop(1, KV, greet_kv, 0)
    lax.fori_loop(1, TP, greet_tp, 0)

    def to_kv(phase, source, target, peer):
        return pltpu.make_async_remote_copy(
            src_ref=source,
            dst_ref=target,
            send_sem=send_sem.at[phase],
            recv_sem=recv_sem.at[phase],
            device_id={"kv": peer},
            device_id_type=MESH,
        )

    def to_tp(phase, source, target, peer):
        return pltpu.make_async_remote_copy(
            src_ref=source,
            dst_ref=target,
            send_sem=send_sem.at[phase],
            recv_sem=recv_sem.at[phase],
            device_id={"tp": peer},
            device_id_type=MESH,
        )

    def all_kv(phase, buffer):
        return to_kv(phase, buffer.at[pl.ds(0, KV - 1)], buffer.at[pl.ds(0, KV - 1)], kv)

    row = lax.broadcasted_iota(jnp.int32, (HD, HD), 0)
    column = lax.broadcasted_iota(jnp.int32, (HD, HD), 1)
    common = row & column
    parity = common
    for shift in (4, 2, 1):
        parity = parity ^ (parity >> shift)
    turn = ((1 - 2 * (parity & 1)).astype(f32) * (1.0 / HD)).astype(bf16)
    loads[0].wait()
    loads[1].wait()
    wide = queries[...].astype(f32)
    heads = jnp.concatenate(
        [wide[:, head * HD : (head + 1) * HD] for head in range(HEADS)], axis=0
    )
    sign = (1 - 2 * signs[...]).astype(f32)
    rotated[kv] = dot((heads * sign).astype(bf16), turn).astype(bf16)

    pl.semaphore_wait(barrier, KV + TP - 2)

    def send_rotated(step, carry):
        to_kv(0, rotated.at[kv], rotated.at[kv], lax.rem(kv + step, KV)).start()
        return carry

    lax.fori_loop(1, KV, send_rotated, 0)

    loads[2].wait()
    loads[3].wait()
    for head in range(HEADS):
        stage[pl.ds(head, KV, stride=HEADS), :] = residual[:, head * HD : (head + 1) * HD].astype(
            f32
        )
    own_residual = stage[pl.ds(pl.multiple_of(kv * HEADS, HEADS), HEADS), :]

    loads[4].wait()
    loads[5].wait()
    all_kv(0, rotated).wait_recv()

    def attend(request):
        query = rotated[request]
        live = count[0, request]
        pages = [table[0, request, slot] for slot in range(SLOTS)]
        scores = [
            jnp.where(
                slot < live,
                lax.dot_general(
                    query, keys[page], (((1,), (1,)), ((), ())), preferred_element_type=f32
                ),
                fill_value,
            )
            for slot, page in enumerate(pages)
        ]
        best = scores[0]
        for score in scores[1:]:
            best = jnp.maximum(best, score)
        best = jnp.max(best, axis=1, keepdims=True)
        weights = [jnp.exp(score - best).astype(bf16) for score in scores]
        total = weights[0].astype(f32)
        for weight in weights[1:]:
            total = total + weight.astype(f32)
        total = jnp.sum(total, axis=1, keepdims=True)
        merged = dot(weights[0], values[pages[0]])
        for weight, page in zip(weights[1:], pages[1:]):
            merged = merged + dot(weight, values[page])
        part_out[request, :, :HD] = (merged / total).astype(bf16)
        part_out[request, :, HD:] = in_lanes(split3(best + jnp.log(total)))

    def send_part(peer):
        to_kv(1, part_out.at[peer], part_in.at[kv], peer).start()

    def attend_block(block, carry):
        peers = [lax.rem(kv + 1 + block * 4 + place, KV) for place in range(4)]
        for peer in peers:
            attend(peer)
        for peer in peers:
            send_part(peer)
        return carry

    lax.fori_loop(0, 3, attend_block, 0)
    peers = [lax.rem(kv + 13 + place, KV) for place in range(4)]
    for peer in peers:
        attend(peer)
    for peer in peers[:3]:
        send_part(peer)
    part_in[kv] = part_out[kv]

    all_kv(1, part_in).wait_recv()
    level = jnp.sum(part_in[:, :, HD:].astype(f32), axis=2, keepdims=True)
    factor = jnp.exp(level - jnp.max(level, axis=0, keepdims=True))
    whole = jnp.sum(factor * part_in[:, :, :HD].astype(f32), axis=0)
    attention = (whole / jnp.sum(factor, axis=0)).astype(bf16)
    attended[kv] = attention

    def send_attended(step, carry):
        to_kv(2, attended.at[kv], attended.at[kv], lax.rem(kv + step, KV)).start()
        return carry

    lax.fori_loop(1, KV, send_attended, 0)
    own_stream = own_residual + attention.astype(f32)

    all_kv(2, attended).wait_recv()
    stage[...] = attended[...].astype(f32).reshape(KV * HEADS, HD)
    squares = jnp.zeros((KV, HD), f32)
    for head in range(HEADS):
        span = slice(head * HD, (head + 1) * HD)
        piece = residual[:, span].astype(f32) + stage[pl.ds(head, KV, stride=HEADS), :]
        squares = squares + piece * piece
        scaled[:, span] = (piece * gain[:, span].astype(f32)).astype(bf16)
    square_out[...] = in_lanes(split3(jnp.sum(squares, axis=1, keepdims=True)))
    square_in[tp] = square_out[...]

    def send_squares(step, carry):
        to_tp(3, square_out, square_in.at[tp], lax.rem(tp + step, TP)).start()
        return carry

    lax.fori_loop(1, TP, send_squares, 0)

    loads[6].wait()
    loads[7].wait()

    def project(step, carry):
        peer = lax.rem(tp + 1 + step, CHUNKS)

        @pl.when(peer < WHOLE)
        def _():
            span = pl.ds(pl.multiple_of(peer * CHUNK, CHUNK), CHUNK)
            sums_out[peer, :, :CHUNK] = dot(scaled[...], gate[:, span]).astype(bf16)
            sums_out[peer, :, CHUNK:] = dot(scaled[...], up[:, span]).astype(bf16)

            @pl.when(peer != tp)
            def _():
                to_tp(4, sums_out.at[peer], sums_in.at[tp], peer).start()

        @pl.when(peer == WHOLE)
        def _():
            sums_out[WHOLE, :, :TAIL] = dot(scaled[...], gate[:, WHOLE * CHUNK :]).astype(bf16)
            sums_out[WHOLE, :, TAIL : 2 * TAIL] = dot(
                scaled[...], up[:, WHOLE * CHUNK :]
            ).astype(bf16)

            @pl.when(peer != tp)
            def _():
                short = pl.ds(0, 2 * TAIL)
                to_tp(
                    7, sums_out.at[WHOLE, :, short], sums_in.at[tp, :, short], WHOLE
                ).start()

        return carry

    lax.fori_loop(0, CHUNKS, project, 0)

    def all_tp(phase, buffer, size):
        return to_tp(phase, buffer.at[pl.ds(0, size)], buffer.at[pl.ds(0, size)], tp)

    all_tp(3, square_in, TP - 1).wait_recv()
    mean = jnp.sum(jnp.sum(square_in[...].astype(f32), axis=0), axis=1, keepdims=True) / (
        FEATURES * TP
    )
    inverse = lax.rsqrt(mean + epsilon)

    def activate(gate_sum, up_sum):
        value = gate_sum * inverse
        return (value / (1.0 + jnp.exp(-value)) * (up_sum * inverse)).astype(bf16)

    @pl.when(tp < WHOLE)
    def _():
        sums_in[tp] = sums_out[tp]
        all_tp(4, sums_in, TP - 1).wait_recv()
        total = jnp.sum(sums_in[...].astype(f32), axis=0)
        hidden[tp] = activate(total[:, :CHUNK], total[:, CHUNK:])

        def send_hidden(step, carry):
            to_tp(5, hidden.at[tp], hidden.at[tp], lax.rem(tp + step, TP)).start()
            return carry

        lax.fori_loop(1, TP, send_hidden, 0)

    @pl.when(tp == WHOLE)
    def _():
        short = pl.ds(0, 2 * TAIL)
        sums_in[WHOLE, :, : 2 * TAIL] = sums_out[WHOLE, :, : 2 * TAIL]
        to_tp(
            7,
            sums_in.at[pl.ds(0, TP - 1), :, short],
            sums_in.at[pl.ds(0, TP - 1), :, short],
            tp,
        ).wait_recv()
        total = jnp.sum(sums_in[:, :, : 2 * TAIL].astype(f32), axis=0)
        hidden[WHOLE, :, :TAIL] = activate(total[:, :TAIL], total[:, TAIL:])

        def send_hidden(step, carry):
            tail = pl.ds(0, TAIL)
            to_tp(
                8,
                hidden.at[WHOLE, :, tail],
                hidden.at[WHOLE, :, tail],
                lax.rem(tp + step, TP),
            ).start()
            return carry

        lax.fori_loop(1, TP, send_hidden, 0)

    loads[8].wait()

    tail_part = hidden.at[WHOLE, :, pl.ds(0, TAIL)]

    @pl.when(tp < WHOLE)
    def _():
        all_tp(5, hidden, WHOLE - 1).wait_recv()
        to_tp(8, tail_part, tail_part, tp).wait_recv()

    @pl.when(tp == WHOLE)
    def _():
        all_tp(5, hidden, WHOLE).wait_recv()

    @pl.when(tp > WHOLE)
    def _():
        all_tp(5, hidden, WHOLE).wait_recv()
        to_tp(8, tail_part, tail_part, tp).wait_recv()

    units = jnp.concatenate(
        [hidden[chunk] for chunk in range(WHOLE)] + [hidden[WHOLE, :, :TAIL]], axis=1
    )

    def contract(block, carry):
        width = 2 * HD
        result = dot(units, down[:, pl.ds(pl.multiple_of(block * width, width), width)])
        stage[pl.ds(2 * block, KV, stride=HEADS), :] = result[:, :HD]
        stage[pl.ds(2 * block + 1, KV, stride=HEADS), :] = result[:, HD:]
        return carry

    lax.fori_loop(0, HEADS // 2, contract, 0)
    mixed_out[...] = stage[...].astype(bf16).reshape(KV, HEADS, HD)
    mixed_in[kv] = mixed_out[kv]

    def send_mixed(step, carry):
        peer = lax.rem(kv + step, KV)
        to_kv(6, mixed_out.at[peer], mixed_in.at[kv], peer).start()
        return carry

    lax.fori_loop(1, KV, send_mixed, 0)
    all_kv(6, mixed_in).wait_recv()
    out[...] = (own_stream + jnp.sum(mixed_in[...].astype(f32), axis=0)).astype(bf16)

    all_kv(0, rotated).wait_send()
    all_kv(1, part_out).wait_send()
    all_kv(2, attended).wait_send()
    all_tp(3, square_in, TP - 1).wait_send()
    all_kv(6, mixed_out).wait_send()
    tail_sums = sums_out.at[WHOLE, :, pl.ds(0, 2 * TAIL)]

    @pl.when(tp < WHOLE)
    def _():
        all_tp(4, sums_out, WHOLE - 1).wait_send()
        to_tp(7, tail_sums, tail_sums, tp).wait_send()
        all_tp(5, sums_out.at[:, :, pl.ds(0, CHUNK)], TP - 1).wait_send()

    @pl.when(tp == WHOLE)
    def _():
        all_tp(4, sums_out, WHOLE).wait_send()
        all_tp(8, sums_out.at[:, :, pl.ds(0, TAIL)], TP - 1).wait_send()

    @pl.when(tp > WHOLE)
    def _():
        all_tp(4, sums_out, WHOLE).wait_send()
        to_tp(7, tail_sums, tail_sums, tp).wait_send()


def shards(
    queries,
    sign_bits,
    key_pages,
    value_pages,
    page_table,
    page_count,
    residual,
    norm_gain,
    gate_weight,
    up_weight,
    down_weight,
):
    anywhere = pl.BlockSpec(memory_space=pl.ANY)
    scalars = pl.BlockSpec(memory_space=pltpu.SMEM)
    result = pl.pallas_call(
        layer,
        out_shape=jax.ShapeDtypeStruct((HEADS, HD), bf16),
        in_specs=[scalars] * 2 + [anywhere] * 9,
        out_specs=pl.BlockSpec(memory_space=pltpu.VMEM),
        scratch_shapes=[
            pltpu.VMEM(queries.shape, bf16),
            pltpu.VMEM((1, HD), jnp.int32),
            pltpu.VMEM(key_pages.shape, bf16),
            pltpu.VMEM(value_pages.shape, bf16),
            pltpu.VMEM(residual.shape, bf16),
            pltpu.VMEM((1, FEATURES), bf16),
            pltpu.VMEM(gate_weight.shape, bf16),
            pltpu.VMEM(up_weight.shape, bf16),
            pltpu.VMEM(down_weight.shape, bf16),
            pltpu.VMEM((KV, HEADS, HD), bf16),
            pltpu.VMEM((KV, HEADS, 2 * HD), bf16),
            pltpu.VMEM((KV, HEADS, 2 * HD), bf16),
            pltpu.VMEM((KV, HEADS, HD), bf16),
            pltpu.VMEM((KV * HEADS, HD), f32),
            pltpu.VMEM((KV, FEATURES), bf16),
            pltpu.VMEM((KV, 128), bf16),
            pltpu.VMEM((TP, KV, 128), bf16),
            pltpu.VMEM((TP, KV, 2 * CHUNK), bf16),
            pltpu.VMEM((TP, KV, 2 * CHUNK), bf16),
            pltpu.VMEM((CHUNKS, KV, CHUNK), bf16),
            pltpu.VMEM((KV, HEADS, HD), bf16),
            pltpu.VMEM((KV, HEADS, HD), bf16),
            pltpu.SemaphoreType.DMA((9,)),
            pltpu.SemaphoreType.DMA((9,)),
            pltpu.SemaphoreType.DMA((9,)),
        ],
        compiler_params=pltpu.CompilerParams(
            collective_id=0, has_side_effects=True, vmem_limit_bytes=48 * 1024 * 1024
        ),
    )(
        page_table,
        page_count,
        queries,
        sign_bits.reshape(1, HD),
        key_pages,
        value_pages,
        residual,
        norm_gain.reshape(1, FEATURES),
        gate_weight,
        up_weight,
        down_weight,
    )
    return result.reshape(1, FEATURES)


def solution(mesh):
    in_specs = (
        P("kv", "tp"),
        P(),
        P("kv", None, "tp"),
        P("kv", None, "tp"),
        P("kv", None, None),
        P("kv", None),
        P(None, "tp"),
        P("tp"),
        P("tp", "kv"),
        P("tp", "kv"),
        P("kv", "tp"),
    )
    out_specs = P("kv", "tp")
    return jax.shard_map(shards, mesh=mesh, in_specs=in_specs, out_specs=out_specs, check_vma=False)
```

```python
from functools import partial

import jax
import jax.numpy as jnp
from jax import lax
from jax.experimental import pallas as pl
from jax.experimental.pallas import tpu as pltpu
from jax.sharding import PartitionSpec as P

fill_value = -1e30
epsilon = 1e-05
f32 = jnp.float32
bf16 = jnp.bfloat16
MESH = pl.DeviceIdType.MESH

KV = 16
TP = 8
HEADS = 16
HD = 128
SLOTS = 4
PAGES = 32
FEATURES = HEADS * HD
UNITS = 1664
CHUNK = 256
CHUNKS = -(-UNITS // CHUNK)
PADDED = CHUNKS * CHUNK


def dot(left, right):
    return jnp.dot(left, right, preferred_element_type=f32)


def split3(value):
    high = value.astype(bf16).astype(f32)
    rest = value - high
    middle = rest.astype(bf16).astype(f32)
    return high, middle, rest - middle


def in_lanes(parts):
    rows = parts[0].shape[0]
    lane = lax.broadcasted_iota(jnp.int32, (rows, 128), 1)
    tile = jnp.zeros((rows, 128), f32)
    for place, part in enumerate(parts):
        tile = jnp.where(lane == place, part, tile)
    return tile.astype(bf16)


def layer(
    table_hbm,
    count_hbm,
    queries_hbm,
    signs_hbm,
    keys_hbm,
    values_hbm,
    residual_hbm,
    gain_hbm,
    gate_hbm,
    up_hbm,
    down_hbm,
    out,
    table,
    count,
    queries,
    signs,
    owner_row,
    owner,
    keys,
    values,
    residual,
    gain,
    gate,
    up,
    down,
    rotated,
    page_max,
    page_total,
    page_out,
    part_out,
    part_in,
    attended,
    stage,
    scaled,
    square_out,
    square_in,
    sums_out,
    sums_in,
    hidden,
    mixed_out,
    mixed_in,
    load_sem,
    send_sem,
    recv_sem,
):
    kv = lax.axis_index("kv")
    tp = lax.axis_index("tp")

    loads = [
        pltpu.make_async_copy(source, target, load_sem.at[place])
        for place, (source, target) in enumerate(
            [
                (queries_hbm, queries),
                (signs_hbm, signs),
                (residual_hbm, residual),
                (gain_hbm, gain),
                (keys_hbm, keys),
                (values_hbm, values),
                (gate_hbm, gate.at[:, pl.ds(0, UNITS)]),
                (up_hbm, up.at[:, pl.ds(0, UNITS)]),
                (down_hbm, down),
                (table_hbm, table),
                (count_hbm, count),
            ]
        )
    ]
    for place in (0, 1, 9, 10, 2, 3, 4, 5, 6, 7, 8):
        loads[place].start()

    x, z = kv // 4, lax.rem(kv, 4)
    offsets = [(dx, dz) for dx in range(4) for dz in range(4) if dx or dz]
    offsets.sort(key=lambda at: -min(at[0], 4 - at[0]) - min(at[1], 4 - at[1]))
    kv_peers = [lax.rem(x + dx, 4) * 4 + lax.rem(z + dz, 4) for dx, dz in offsets]
    tp_peers = [lax.rem(tp + step, TP) for step in (4, 5, 3, 2, 6, 7, 1)]

    barrier = pltpu.get_barrier_semaphore()
    for peer in kv_peers:
        pl.semaphore_signal(barrier, inc=1, device_id={"kv": peer}, device_id_type=MESH)
    for peer in tp_peers:
        pl.semaphore_signal(barrier, inc=1, device_id={"tp": peer}, device_id_type=MESH)

    def to_kv(phase, source, target, peer):
        return pltpu.make_async_remote_copy(
            src_ref=source,
            dst_ref=target,
            send_sem=send_sem.at[phase],
            recv_sem=recv_sem.at[phase],
            device_id={"kv": peer},
            device_id_type=MESH,
        )

    def to_tp(phase, source, target, peer):
        return pltpu.make_async_remote_copy(
            src_ref=source,
            dst_ref=target,
            send_sem=send_sem.at[phase],
            recv_sem=recv_sem.at[phase],
            device_id={"tp": peer},
            device_id_type=MESH,
        )

    def all_kv(phase, buffer):
        return to_kv(phase, buffer.at[pl.ds(0, KV - 1)], buffer.at[pl.ds(0, KV - 1)], kv)

    row = lax.broadcasted_iota(jnp.int32, (HD, HD), 0)
    column = lax.broadcasted_iota(jnp.int32, (HD, HD), 1)
    common = row & column
    parity = common
    for shift in (4, 2, 1):
        parity = parity ^ (parity >> shift)
    turn = ((1 - 2 * (parity & 1)).astype(f32) * (1.0 / HD)).astype(bf16)
    loads[0].wait()
    loads[1].wait()
    wide = queries[...].astype(f32)
    heads = jnp.concatenate(
        [wide[:, head * HD : (head + 1) * HD] for head in range(HEADS)], axis=0
    )
    sign = (1 - 2 * signs[...]).astype(f32)
    rotated[kv] = dot((heads * sign).astype(bf16), turn).astype(bf16)

    loads[9].wait()
    loads[10].wait()
    page_lane = lax.broadcasted_iota(jnp.int32, (1, 128), 1)
    owners = jnp.zeros((1, 128), jnp.int32)
    for request in range(KV):
        for slot in range(SLOTS):
            page = jnp.where(slot < count[0, request], table[0, slot, request], -1)
            owners = jnp.where(page_lane == page, request, owners)
    owner_row[...] = owners
    owner_copy = pltpu.make_async_copy(owner_row, owner, load_sem.at[11])
    owner_copy.start()
    gate[:, UNITS:] = jnp.zeros((FEATURES, PADDED - UNITS), bf16)
    up[:, UNITS:] = jnp.zeros((FEATURES, PADDED - UNITS), bf16)

    pl.semaphore_wait(barrier, KV + TP - 2)

    for peer in kv_peers:
        to_kv(0, rotated.at[kv], rotated.at[kv], peer).start()

    loads[2].wait()
    loads[3].wait()
    for head in range(HEADS):
        stage[pl.ds(head, KV, stride=HEADS), :] = residual[:, head * HD : (head + 1) * HD].astype(
            f32
        )
    own_residual = stage[pl.ds(pl.multiple_of(kv * HEADS, HEADS), HEADS), :]

    owner_copy.wait()
    loads[4].wait()
    loads[5].wait()
    all_kv(0, rotated).wait_recv()

    pages = range(PAGES)
    scores = [
        lax.dot_general(
            rotated[owner[0, page]],
            keys[page],
            (((1,), (1,)), ((), ())),
            preferred_element_type=f32,
        )
        for page in pages
    ]
    largest = [jnp.max(score, axis=1, keepdims=True) for score in scores]
    weights = [jnp.exp(score - best).astype(bf16) for score, best in zip(scores, largest)]
    totals = [jnp.sum(weight.astype(f32), axis=1, keepdims=True) for weight in weights]
    outs = [dot(weight, values[page]) for page, weight in zip(pages, weights)]
    for page in pages:
        page_max[page] = jnp.broadcast_to(largest[page], (HEADS, HD))
        page_total[page] = jnp.broadcast_to(totals[page], (HEADS, HD))
        page_out[page] = outs[page]

    parts = []
    for request in range(KV):
        owned = [table[0, slot, request] for slot in range(SLOTS)]
        live = count[0, request]
        tops = [
            jnp.where(slot < live, page_max[page], fill_value) for slot, page in enumerate(owned)
        ]
        best = jnp.maximum(jnp.maximum(tops[0], tops[1]), jnp.maximum(tops[2], tops[3]))
        factors = [jnp.exp(top - best) for top in tops]
        total = sum(factor * page_total[page] for factor, page in zip(factors, owned))
        merged = sum(factor * page_out[page] for factor, page in zip(factors, owned))
        parts.append(((merged / total).astype(bf16), in_lanes(split3(best + jnp.log(total)))))
    for request, (value, level) in enumerate(parts):
        part_out[request, :, :HD] = value
        part_out[request, :, HD:] = level
    for peer in kv_peers:
        to_kv(1, part_out.at[peer], part_in.at[kv], peer).start()
    part_in[kv] = part_out[kv]

    all_kv(1, part_in).wait_recv()
    level = jnp.sum(part_in[:, :, HD:].astype(f32), axis=2, keepdims=True)
    factor = jnp.exp(level - jnp.max(level, axis=0, keepdims=True))
    whole = jnp.sum(factor * part_in[:, :, :HD].astype(f32), axis=0)
    attention = (whole / jnp.sum(factor, axis=0)).astype(bf16)
    attended[kv] = attention

    for peer in kv_peers:
        to_kv(2, attended.at[kv], attended.at[kv], peer).start()
    own_stream = own_residual + attention.astype(f32)

    all_kv(2, attended).wait_recv()
    stage[...] = attended[...].astype(f32).reshape(KV * HEADS, HD)
    squares = jnp.zeros((KV, HD), f32)
    for head in range(HEADS):
        span = slice(head * HD, (head + 1) * HD)
        piece = residual[:, span].astype(f32) + stage[pl.ds(head, KV, stride=HEADS), :]
        squares = squares + piece * piece
        scaled[:, span] = (piece * gain[span].astype(f32)[None, :]).astype(bf16)
    square_out[...] = in_lanes(split3(jnp.sum(squares, axis=1, keepdims=True)))
    square_in[tp] = square_out[...]

    for peer in tp_peers:
        to_tp(3, square_out, square_in.at[tp], peer).start()

    loads[6].wait()
    loads[7].wait()

    for step in range(CHUNKS):
        peer = lax.rem(tp + 1 + step, CHUNKS)
        span = pl.ds(pl.multiple_of(peer * CHUNK, CHUNK), CHUNK)
        sums_out[peer, :, :CHUNK] = dot(scaled[...], gate[:, span]).astype(bf16)
        sums_out[peer, :, CHUNK:] = dot(scaled[...], up[:, span]).astype(bf16)
        if step < CHUNKS - 1:
            to_tp(4, sums_out.at[peer], sums_in.at[tp], peer).start()

    @pl.when(tp == CHUNKS)
    def _():
        to_tp(4, sums_out.at[0], sums_in.at[tp], 0).start()

    def all_tp(phase, buffer, size):
        return to_tp(phase, buffer.at[pl.ds(0, size)], buffer.at[pl.ds(0, size)], tp)

    all_tp(3, square_in, TP - 1).wait_recv()
    mean = jnp.sum(jnp.sum(square_in[...].astype(f32), axis=0), axis=1, keepdims=True) / (
        FEATURES * TP
    )
    inverse = lax.rsqrt(mean + epsilon)

    def activate(gate_sum, up_sum):
        value = gate_sum * inverse
        return (value / (1.0 + jnp.exp(-value)) * (up_sum * inverse)).astype(bf16)

    @pl.when(tp < CHUNKS)
    def _():
        sums_in[tp] = sums_out[tp]
        all_tp(4, sums_in, TP - 1).wait_recv()
        total = jnp.sum(sums_in[...].astype(f32), axis=0)
        hidden[tp] = activate(total[:, :CHUNK], total[:, CHUNK:])
        for peer in tp_peers:
            to_tp(5, hidden.at[tp], hidden.at[tp], peer).start()

    loads[8].wait()

    @pl.when(tp < CHUNKS)
    def _():
        all_tp(5, hidden, CHUNKS - 1).wait_recv()

    @pl.when(tp == CHUNKS)
    def _():
        all_tp(5, hidden, CHUNKS).wait_recv()

    units = jnp.concatenate([hidden[chunk] for chunk in range(CHUNKS)], axis=1)[:, :UNITS]
    result = dot(units, down[...])
    for head in range(HEADS):
        stage[pl.ds(head, KV, stride=HEADS), :] = result[:, head * HD : (head + 1) * HD]
    mixed_out[...] = stage[...].astype(bf16).reshape(KV, HEADS, HD)
    for peer in kv_peers:
        to_kv(6, mixed_out.at[peer], mixed_in.at[kv], peer).start()
    mixed_in[kv] = mixed_out[kv]
    all_kv(6, mixed_in).wait_recv()
    out[...] = (own_stream + jnp.sum(mixed_in[...].astype(f32), axis=0)).astype(bf16)

    all_kv(0, rotated).wait_send()
    all_kv(1, part_out).wait_send()
    all_kv(2, attended).wait_send()
    all_tp(3, square_in, TP - 1).wait_send()
    all_kv(6, mixed_out).wait_send()

    @pl.when(tp < CHUNKS)
    def _():
        all_tp(4, sums_out, CHUNKS - 1).wait_send()
        all_tp(5, sums_out.at[:, :, pl.ds(0, CHUNK)], TP - 1).wait_send()

    @pl.when(tp == CHUNKS)
    def _():
        all_tp(4, sums_out, CHUNKS).wait_send()


def shards(
    queries,
    sign_bits,
    key_pages,
    value_pages,
    page_table,
    page_count,
    residual,
    norm_gain,
    gate_weight,
    up_weight,
    down_weight,
):
    in_hbm = pl.BlockSpec(memory_space=pltpu.HBM)
    result = pl.pallas_call(
        layer,
        out_shape=jax.ShapeDtypeStruct((HEADS, HD), bf16),
        in_specs=[in_hbm] * 11,
        out_specs=pl.BlockSpec(memory_space=pltpu.VMEM),
        scratch_shapes=[
            pltpu.SMEM((1, SLOTS, KV), jnp.int32),
            pltpu.SMEM((1, KV), jnp.int32),
            pltpu.VMEM(queries.shape, bf16),
            pltpu.VMEM((1, HD), jnp.int32),
            pltpu.VMEM((1, 128), jnp.int32),
            pltpu.SMEM((1, 128), jnp.int32),
            pltpu.VMEM(key_pages.shape, bf16),
            pltpu.VMEM(value_pages.shape, bf16),
            pltpu.VMEM(residual.shape, bf16),
            pltpu.VMEM((FEATURES,), bf16),
            pltpu.VMEM((FEATURES, PADDED), bf16),
            pltpu.VMEM((FEATURES, PADDED), bf16),
            pltpu.VMEM(down_weight.shape, bf16),
            pltpu.VMEM((KV, HEADS, HD), bf16),
            pltpu.VMEM((PAGES, HEADS, HD), f32),
            pltpu.VMEM((PAGES, HEADS, HD), f32),
            pltpu.VMEM((PAGES, HEADS, HD), f32),
            pltpu.VMEM((KV, HEADS, 2 * HD), bf16),
            pltpu.VMEM((KV, HEADS, 2 * HD), bf16),
            pltpu.VMEM((KV, HEADS, HD), bf16),
            pltpu.VMEM((KV * HEADS, HD), f32),
            pltpu.VMEM((KV, FEATURES), bf16),
            pltpu.VMEM((KV, 128), bf16),
            pltpu.VMEM((TP, KV, 128), bf16),
            pltpu.VMEM((CHUNKS, KV, 2 * CHUNK), bf16),
            pltpu.VMEM((TP, KV, 2 * CHUNK), bf16),
            pltpu.VMEM((CHUNKS, KV, CHUNK), bf16),
            pltpu.VMEM((KV, HEADS, HD), bf16),
            pltpu.VMEM((KV, HEADS, HD), bf16),
            pltpu.SemaphoreType.DMA((12,)),
            pltpu.SemaphoreType.DMA((7,)),
            pltpu.SemaphoreType.DMA((7,)),
        ],
        compiler_params=pltpu.CompilerParams(
            collective_id=0, has_side_effects=True, vmem_limit_bytes=63 * 1024 * 1024
        ),
    )(
        jnp.transpose(page_table, (0, 2, 1)),
        page_count,
        queries,
        sign_bits.reshape(1, HD),
        key_pages,
        value_pages,
        residual,
        norm_gain,
        gate_weight,
        up_weight,
        down_weight,
    )
    return result.reshape(1, FEATURES)


def solution(mesh):
    in_specs = (
        P("kv", "tp"),
        P(),
        P("kv", None, "tp"),
        P("kv", None, "tp"),
        P("kv", None, None),
        P("kv", None),
        P(None, "tp"),
        P("tp"),
        P("tp", "kv"),
        P("tp", "kv"),
        P("kv", "tp"),
    )
    out_specs = P("kv", "tp")
    return jax.shard_map(shards, mesh=mesh, in_specs=in_specs, out_specs=out_specs, check_vma=False)
```

```python
from functools import partial

import jax
import jax.numpy as jnp
from jax import lax
from jax.experimental import pallas as pl
from jax.experimental.pallas import tpu as pltpu
from jax.sharding import PartitionSpec as P

fill_value = -1e30
epsilon = 1e-05
f32 = jnp.float32
bf16 = jnp.bfloat16
MESH = pl.DeviceIdType.MESH

KV = 16
TP = 8
HEADS = 16
HD = 128
SLOTS = 4
PAGES = 32
FEATURES = HEADS * HD
UNITS = 1664
CHUNK = 256
CHUNKS = -(-UNITS // CHUNK)
PADDED = CHUNKS * CHUNK


def dot(left, right):
    return jnp.dot(left, right, preferred_element_type=f32)


def pair_of(kv):
    x, z = kv // 4, kv % 4
    return (x % 2) * 4 + (z + 2 * (x // 2)) % 4, x // 2


def split3(value):
    high = value.astype(bf16).astype(f32)
    rest = value - high
    middle = rest.astype(bf16).astype(f32)
    return high, middle, rest - middle


def in_lanes(parts):
    rows = parts[0].shape[0]
    lane = lax.broadcasted_iota(jnp.int32, (rows, 128), 1)
    tile = jnp.zeros((rows, 128), f32)
    for place, part in enumerate(parts):
        tile = jnp.where(lane == place, part, tile)
    return tile.astype(bf16)


def layer(
    table_hbm,
    count_hbm,
    queries_hbm,
    signs_hbm,
    keys_hbm,
    values_hbm,
    residual_hbm,
    gain_hbm,
    gate_hbm,
    up_hbm,
    down_hbm,
    out,
    table,
    count,
    queries,
    signs,
    owner_row,
    owner,
    keys,
    values,
    residual,
    gain,
    gate,
    up,
    down,
    rotated,
    page_max,
    page_total,
    page_out,
    level_out,
    level_in,
    part_out,
    part_in,
    attended,
    stage,
    scaled,
    square_out,
    square_in,
    sums_out,
    sums_in,
    hidden,
    mixed_out,
    mixed_in,
    load_sem,
    send_sem,
    recv_sem,
):
    kv = lax.axis_index("kv")
    tp = lax.axis_index("tp")

    loads = [
        pltpu.make_async_copy(source, target, load_sem.at[place])
        for place, (source, target) in enumerate(
            [
                (queries_hbm, queries),
                (signs_hbm, signs),
                (residual_hbm, residual),
                (gain_hbm, gain),
                (keys_hbm, keys),
                (values_hbm, values),
                (gate_hbm, gate.at[:, pl.ds(0, UNITS)]),
                (up_hbm, up.at[:, pl.ds(0, UNITS)]),
                (down_hbm, down),
                (table_hbm, table),
                (count_hbm, count),
            ]
        )
    ]
    for place in (0, 1, 9, 10, 2, 3, 4, 5, 6, 7, 8):
        loads[place].start()

    x, z = kv // 4, lax.rem(kv, 4)
    offsets = [(dx, dz) for dx in range(4) for dz in range(4) if dx or dz]
    offsets.sort(key=lambda at: -min(at[0], 4 - at[0]) - min(at[1], 4 - at[1]))
    kv_peers = [lax.rem(x + dx, 4) * 4 + lax.rem(z + dz, 4) for dx, dz in offsets]
    pair, member = pair_of(kv)
    near = [(0, 2), (1, 1), (1, 3), (0, 1), (0, 3), (1, 0), (3, 0)]
    near_peers = [lax.rem(x + dx, 4) * 4 + lax.rem(z + dz, 4) for dx, dz in near]

    y, core = tp // 2, tp % 2
    row = [
        lax.rem(y + dy, 4) * 2 + side
        for dy in (2, 1, 3, 0)
        for side in ((core, 1 - core) if dy else (1 - core, core))
    ]
    tp_peers = row[:-1]
    gap = sum(jnp.where(peer == TP - 1, place, 0) for place, peer in enumerate(row))
    chunk_order = [
        jnp.where(place < gap, row[place], row[place + 1]) for place in range(CHUNKS)
    ]

    barrier = pltpu.get_barrier_semaphore()
    for peer in kv_peers:
        pl.semaphore_signal(barrier, inc=1, device_id={"kv": peer}, device_id_type=MESH)
    for peer in tp_peers:
        pl.semaphore_signal(barrier, inc=1, device_id={"tp": peer}, device_id_type=MESH)

    def to_kv(phase, source, target, peer):
        return pltpu.make_async_remote_copy(
            src_ref=source,
            dst_ref=target,
            send_sem=send_sem.at[phase],
            recv_sem=recv_sem.at[phase],
            device_id={"kv": peer},
            device_id_type=MESH,
        )

    def to_tp(phase, source, target, peer):
        return pltpu.make_async_remote_copy(
            src_ref=source,
            dst_ref=target,
            send_sem=send_sem.at[phase],
            recv_sem=recv_sem.at[phase],
            device_id={"tp": peer},
            device_id_type=MESH,
        )

    def all_kv(phase, buffer):
        return to_kv(phase, buffer.at[pl.ds(0, KV - 1)], buffer.at[pl.ds(0, KV - 1)], kv)

    row = lax.broadcasted_iota(jnp.int32, (HD, HD), 0)
    column = lax.broadcasted_iota(jnp.int32, (HD, HD), 1)
    common = row & column
    parity = common
    for shift in (4, 2, 1):
        parity = parity ^ (parity >> shift)
    turn = ((1 - 2 * (parity & 1)).astype(f32) * (1.0 / HD)).astype(bf16)
    loads[0].wait()
    loads[1].wait()
    wide = queries[...].astype(f32)
    heads = jnp.concatenate(
        [wide[:, head * HD : (head + 1) * HD] for head in range(HEADS)], axis=0
    )
    sign = (1 - 2 * signs[...]).astype(f32)
    rotated[kv] = dot((heads * sign).astype(bf16), turn).astype(bf16)

    loads[9].wait()
    loads[10].wait()
    page_lane = lax.broadcasted_iota(jnp.int32, (1, 128), 1)
    owners = jnp.zeros((1, 128), jnp.int32)
    for request in range(KV):
        for slot in range(SLOTS):
            page = jnp.where(slot < count[0, request], table[0, slot, request], -1)
            owners = jnp.where(page_lane == page, request, owners)
    owner_row[...] = owners
    owner_copy = pltpu.make_async_copy(owner_row, owner, load_sem.at[11])
    owner_copy.start()
    gate[:, UNITS:] = jnp.zeros((FEATURES, PADDED - UNITS), bf16)
    up[:, UNITS:] = jnp.zeros((FEATURES, PADDED - UNITS), bf16)

    pl.semaphore_wait(barrier, KV + TP - 2)

    for peer in kv_peers:
        to_kv(0, rotated.at[kv], rotated.at[kv], peer).start()

    loads[2].wait()
    loads[3].wait()
    for head in range(HEADS):
        stage[pl.ds(head, KV, stride=HEADS), :] = residual[:, head * HD : (head + 1) * HD].astype(
            f32
        )
    own_residual = stage[pl.ds(pl.multiple_of(kv * HEADS, HEADS), HEADS), :]

    owner_copy.wait()
    loads[4].wait()
    loads[5].wait()
    all_kv(0, rotated).wait_recv()

    pages = range(PAGES)
    scores = [
        lax.dot_general(
            rotated[owner[0, page]],
            keys[page],
            (((1,), (1,)), ((), ())),
            preferred_element_type=f32,
        )
        for page in pages
    ]
    largest = [jnp.max(score, axis=1, keepdims=True) for score in scores]
    weights = [jnp.exp(score - best).astype(bf16) for score, best in zip(scores, largest)]
    totals = [jnp.sum(weight.astype(f32), axis=1, keepdims=True) for weight in weights]
    for page in pages:
        page_max[page] = jnp.broadcast_to(largest[page], (HEADS, HD))
        page_total[page] = jnp.broadcast_to(totals[page], (HEADS, HD))

    lane = lax.broadcasted_iota(jnp.int32, (HEADS, 128), 1)
    levels = jnp.zeros((HEADS, 128), f32)
    owned = [[table[0, slot, request] for slot in range(SLOTS)] for request in range(KV)]
    shares = []
    for request in range(KV):
        live = count[0, request]
        tops = [
            jnp.where(slot < live, page_max[page], fill_value)
            for slot, page in enumerate(owned[request])
        ]
        best = jnp.maximum(jnp.maximum(tops[0], tops[1]), jnp.maximum(tops[2], tops[3]))
        factors = [jnp.exp(top - best) for top in tops]
        total = sum(factor * page_total[page] for factor, page in zip(factors, owned[request]))
        shares.append([factor / total for factor in factors])
        which, place = pair_of(request)
        for part, value in enumerate(split3(best + jnp.log(total))):
            levels = jnp.where(lane == part * KV + 2 * which + place, value, levels)
    level_out[...] = levels.astype(bf16)
    for peer in kv_peers:
        to_kv(7, level_out, level_in.at[kv], peer).start()
    level_in[kv] = level_out[...]

    outs = [dot(weight, values[page]) for page, weight in zip(pages, weights)]
    for page in pages:
        page_out[page] = outs[page]
    merged = [
        sum(share * page_out[page] for share, page in zip(shares[request], owned[request]))
        for request in range(KV)
    ]
    for request in range(KV):
        which, place = pair_of(request)
        part_out[which, place] = merged[request].astype(bf16)
    for peer in kv_peers:
        to_kv(1, part_out.at[pair_of(peer)[0]], part_in.at[kv], peer).start()
    part_in[kv] = part_out[pair]

    picked_lane = lax.broadcasted_iota(jnp.int32, (128, 2 * HD), 0)
    picked_column = lax.broadcasted_iota(jnp.int32, (128, 2 * HD), 1)
    pick = (
        (picked_lane < 3 * KV)
        & (lax.rem(picked_lane, KV) == 2 * pair + jnp.where(picked_column < HD, 0, 1))
    ).astype(f32).astype(bf16)
    all_kv(7, level_in).wait_recv()
    level = dot(level_in[...].reshape(KV * HEADS, 128), pick).reshape(KV, HEADS, 2 * HD)
    factor = jnp.exp(level - jnp.max(level, axis=0, keepdims=True))
    whole = jnp.sum(factor, axis=0)
    factor = factor / whole[None]
    all_kv(1, part_in).wait_recv()
    both = [
        jnp.sum(factor[:, :, place * HD : (place + 1) * HD] * part_in[:, place].astype(f32), axis=0)
        for place in range(2)
    ]
    for place in range(2):
        attended[pair, place] = both[place].astype(bf16)
    for peer in near_peers:
        to_kv(2, attended.at[pair], attended.at[pair], peer).start()
    attention = jnp.where(member == 0, both[0], both[1]).astype(bf16)
    own_stream = own_residual + attention.astype(f32)

    def near_kv(phase, buffer):
        return to_kv(phase, buffer.at[pl.ds(0, 7)], buffer.at[pl.ds(0, 7)], kv)

    near_kv(2, attended).wait_recv()
    for request in range(KV):
        which, place = pair_of(request)
        stage[request * HEADS : (request + 1) * HEADS, :] = attended[which, place].astype(f32)
    squares = jnp.zeros((KV, HD), f32)
    for head in range(HEADS):
        span = slice(head * HD, (head + 1) * HD)
        piece = residual[:, span].astype(f32) + stage[pl.ds(head, KV, stride=HEADS), :]
        squares = squares + piece * piece
        scaled[:, span] = (piece * gain[span].astype(f32)[None, :]).astype(bf16)
    square_out[...] = in_lanes(split3(jnp.sum(squares, axis=1, keepdims=True)))
    square_in[tp] = square_out[...]

    for peer in tp_peers:
        to_tp(3, square_out, square_in.at[tp], peer).start()

    loads[6].wait()
    loads[7].wait()

    for step, peer in enumerate(chunk_order):
        span = pl.ds(pl.multiple_of(peer * CHUNK, CHUNK), CHUNK)
        sums_out[peer, :, :CHUNK] = dot(scaled[...], gate[:, span]).astype(bf16)
        sums_out[peer, :, CHUNK:] = dot(scaled[...], up[:, span]).astype(bf16)
        if step < CHUNKS - 1:
            to_tp(4, sums_out.at[peer], sums_in.at[tp], peer).start()

    @pl.when(tp == CHUNKS)
    def _():
        to_tp(4, sums_out.at[CHUNKS - 1], sums_in.at[tp], CHUNKS - 1).start()

    def all_tp(phase, buffer, size):
        return to_tp(phase, buffer.at[pl.ds(0, size)], buffer.at[pl.ds(0, size)], tp)

    all_tp(3, square_in, TP - 1).wait_recv()
    mean = jnp.sum(jnp.sum(square_in[...].astype(f32), axis=0), axis=1, keepdims=True) / (
        FEATURES * TP
    )
    inverse = lax.rsqrt(mean + epsilon)

    def activate(gate_sum, up_sum):
        value = gate_sum * inverse
        return (value / (1.0 + jnp.exp(-value)) * (up_sum * inverse)).astype(bf16)

    @pl.when(tp < CHUNKS)
    def _():
        sums_in[tp] = sums_out[tp]
        all_tp(4, sums_in, TP - 1).wait_recv()
        total = jnp.sum(sums_in[...].astype(f32), axis=0)
        hidden[tp] = activate(total[:, :CHUNK], total[:, CHUNK:])
        for peer in tp_peers:
            to_tp(5, hidden.at[tp], hidden.at[tp], peer).start()

    loads[8].wait()

    @pl.when(tp < CHUNKS)
    def _():
        all_tp(5, hidden, CHUNKS - 1).wait_recv()

    @pl.when(tp == CHUNKS)
    def _():
        all_tp(5, hidden, CHUNKS).wait_recv()

    units = jnp.concatenate([hidden[chunk] for chunk in range(CHUNKS)], axis=1)[:, :UNITS]
    result = dot(units, down[...])
    for head in range(HEADS):
        stage[pl.ds(head, KV, stride=HEADS), :] = result[:, head * HD : (head + 1) * HD]
    mixed_out[...] = stage[...].astype(bf16).reshape(KV, HEADS, HD)
    for peer in kv_peers:
        to_kv(6, mixed_out.at[peer], mixed_in.at[kv], peer).start()
    mixed_in[kv] = mixed_out[kv]
    all_kv(6, mixed_in).wait_recv()
    out[...] = (own_stream + jnp.sum(mixed_in[...].astype(f32), axis=0)).astype(bf16)

    all_kv(0, rotated).wait_send()
    all_kv(1, part_in).wait_send()
    near_kv(2, attended).wait_send()
    all_kv(7, level_in).wait_send()
    all_tp(3, square_in, TP - 1).wait_send()
    all_kv(6, mixed_out).wait_send()

    @pl.when(tp < CHUNKS)
    def _():
        all_tp(4, sums_out, CHUNKS - 1).wait_send()
        all_tp(5, sums_out.at[:, :, pl.ds(0, CHUNK)], TP - 1).wait_send()

    @pl.when(tp == CHUNKS)
    def _():
        all_tp(4, sums_out, CHUNKS).wait_send()


def shards(
    queries,
    sign_bits,
    key_pages,
    value_pages,
    page_table,
    page_count,
    residual,
    norm_gain,
    gate_weight,
    up_weight,
    down_weight,
):
    in_hbm = pl.BlockSpec(memory_space=pltpu.HBM)
    result = pl.pallas_call(
        layer,
        out_shape=pltpu.VMEM((HEADS, HD), bf16),
        in_specs=[in_hbm] * 11,
        out_specs=pl.BlockSpec(memory_space=pltpu.VMEM),
        scratch_shapes=[
            pltpu.SMEM((1, SLOTS, KV), jnp.int32),
            pltpu.SMEM((1, KV), jnp.int32),
            pltpu.VMEM(queries.shape, bf16),
            pltpu.VMEM((1, HD), jnp.int32),
            pltpu.VMEM((1, 128), jnp.int32),
            pltpu.SMEM((1, 128), jnp.int32),
            pltpu.VMEM(key_pages.shape, bf16),
            pltpu.VMEM(value_pages.shape, bf16),
            pltpu.VMEM(residual.shape, bf16),
            pltpu.VMEM((FEATURES,), bf16),
            pltpu.VMEM((FEATURES, PADDED), bf16),
            pltpu.VMEM((FEATURES, PADDED), bf16),
            pltpu.VMEM(down_weight.shape, bf16),
            pltpu.VMEM((KV, HEADS, HD), bf16),
            pltpu.VMEM((PAGES, HEADS, HD), f32),
            pltpu.VMEM((PAGES, HEADS, HD), f32),
            pltpu.VMEM((PAGES, HEADS, HD), f32),
            pltpu.VMEM((HEADS, 128), bf16),
            pltpu.VMEM((KV, HEADS, 128), bf16),
            pltpu.VMEM((KV // 2, 2, HEADS, HD), bf16),
            pltpu.VMEM((KV, 2, HEADS, HD), bf16),
            pltpu.VMEM((KV // 2, 2, HEADS, HD), bf16),
            pltpu.VMEM((KV * HEADS, HD), f32),
            pltpu.VMEM((KV, FEATURES), bf16),
            pltpu.VMEM((KV, 128), bf16),
            pltpu.VMEM((TP, KV, 128), bf16),
            pltpu.VMEM((CHUNKS, KV, 2 * CHUNK), bf16),
            pltpu.VMEM((TP, KV, 2 * CHUNK), bf16),
            pltpu.VMEM((CHUNKS, KV, CHUNK), bf16),
            pltpu.VMEM((KV, HEADS, HD), bf16),
            pltpu.VMEM((KV, HEADS, HD), bf16),
            pltpu.SemaphoreType.DMA((12,)),
            pltpu.SemaphoreType.DMA((8,)),
            pltpu.SemaphoreType.DMA((8,)),
        ],
        compiler_params=pltpu.CompilerParams(
            collective_id=0, has_side_effects=True, vmem_limit_bytes=63 * 1024 * 1024
        ),
    )(
        jnp.transpose(page_table, (0, 2, 1)),
        page_count,
        queries,
        sign_bits.reshape(1, HD),
        key_pages,
        value_pages,
        residual,
        norm_gain,
        gate_weight,
        up_weight,
        down_weight,
    )
    return result.reshape(1, FEATURES)


def solution(mesh):
    in_specs = (
        P("kv", "tp"),
        P(),
        P("kv", None, "tp"),
        P("kv", None, "tp"),
        P("kv", None, None),
        P("kv", None),
        P(None, "tp"),
        P("tp"),
        P("tp", "kv"),
        P("tp", "kv"),
        P("kv", "tp"),
    )
    out_specs = P("kv", "tp")
    return jax.shard_map(shards, mesh=mesh, in_specs=in_specs, out_specs=out_specs, check_vma=False)
```

```python
from functools import partial

import jax
import jax.numpy as jnp
from jax import lax
from jax.experimental import pallas as pl
from jax.experimental.pallas import tpu as pltpu
from jax.sharding import PartitionSpec as P

fill_value = -1e30
epsilon = 1e-05
f32 = jnp.float32
bf16 = jnp.bfloat16
MESH = pl.DeviceIdType.MESH

KV = 16
TP = 8
HEADS = 16
HD = 128
SLOTS = 4
PAGES = 32
FEATURES = HEADS * HD
UNITS = 1664
CHUNK = 256
CHUNKS = -(-UNITS // CHUNK)
PADDED = CHUNKS * CHUNK


def dot(left, right):
    return jnp.dot(left, right, preferred_element_type=f32)


def pair_of(kv):
    x, z = kv // 4, kv % 4
    return (x % 2) * 4 + (z + 2 * (x // 2)) % 4, x // 2


def split3(value):
    high = value.astype(bf16).astype(f32)
    rest = value - high
    middle = rest.astype(bf16).astype(f32)
    return high, middle, rest - middle


def in_lanes(parts):
    rows = parts[0].shape[0]
    lane = lax.broadcasted_iota(jnp.int32, (rows, 128), 1)
    tile = jnp.zeros((rows, 128), f32)
    for place, part in enumerate(parts):
        tile = jnp.where(lane == place, part, tile)
    return tile.astype(bf16)


def layer(
    table_hbm,
    count_hbm,
    queries_hbm,
    signs_hbm,
    keys_hbm,
    values_hbm,
    residual_hbm,
    gain_hbm,
    gate_hbm,
    up_hbm,
    down_hbm,
    out,
    table,
    count,
    queries,
    signs,
    owner_row,
    owner,
    keys,
    values,
    residual,
    gain,
    gate,
    up,
    down,
    rotated,
    page_max,
    page_total,
    page_out,
    level_out,
    level_in,
    part_out,
    part_in,
    attended,
    stage,
    scaled,
    square_out,
    square_in,
    sums_out,
    sums_in,
    hidden,
    product,
    mixed_out,
    mixed_in,
    load_sem,
    send_sem,
    recv_sem,
):
    kv = lax.axis_index("kv")
    tp = lax.axis_index("tp")

    loads = [
        pltpu.make_async_copy(source, target, load_sem.at[place])
        for place, (source, target) in enumerate(
            [
                (queries_hbm, queries),
                (signs_hbm, signs),
                (residual_hbm, residual),
                (gain_hbm, gain),
                (keys_hbm, keys),
                (values_hbm, values),
                (gate_hbm, gate.at[:, pl.ds(0, UNITS)]),
                (up_hbm, up.at[:, pl.ds(0, UNITS)]),
                (down_hbm, down.at[pl.ds(0, UNITS)]),
                (table_hbm, table),
                (count_hbm, count),
            ]
        )
    ]
    loads[0].start()
    loads[1].start()

    x, z = kv // 4, lax.rem(kv, 4)
    offsets = [(dx, dz) for dx in range(4) for dz in range(4) if dx or dz]
    offsets.sort(key=lambda at: -min(at[0], 4 - at[0]) - min(at[1], 4 - at[1]))
    kv_peers = [lax.rem(x + dx, 4) * 4 + lax.rem(z + dz, 4) for dx, dz in offsets]
    pair, member = pair_of(kv)
    near = [(0, 2), (1, 1), (3, 1), (0, 1), (0, 3), (1, 0), (3, 0)]
    near_peers = [lax.rem(x + dx, 4) * 4 + lax.rem(z + dz, 4) for dx, dz in near]

    y, core = tp // 2, tp % 2
    row = [
        lax.rem(y + dy, 4) * 2 + side
        for dy in (2, 1, 3, 0)
        for side in ((core, 1 - core) if dy else (1 - core, core))
    ]
    tp_peers = row[:-1]
    gap = sum(jnp.where(peer == TP - 1, place, 0) for place, peer in enumerate(row))
    chunk_order = [
        jnp.where(place < gap, row[place], row[place + 1]) for place in range(CHUNKS)
    ]

    barrier = pltpu.get_barrier_semaphore()
    for peer in kv_peers:
        pl.semaphore_signal(barrier, inc=1, device_id={"kv": peer}, device_id_type=MESH)
    for peer in tp_peers:
        pl.semaphore_signal(barrier, inc=1, device_id={"tp": peer}, device_id_type=MESH)

    for place in (9, 10, 2, 3, 4, 5, 6, 7, 8):
        loads[place].start()

    def to_kv(phase, source, target, peer):
        return pltpu.make_async_remote_copy(
            src_ref=source,
            dst_ref=target,
            send_sem=send_sem.at[phase],
            recv_sem=recv_sem.at[phase],
            device_id={"kv": peer},
            device_id_type=MESH,
        )

    def to_tp(phase, source, target, peer):
        return pltpu.make_async_remote_copy(
            src_ref=source,
            dst_ref=target,
            send_sem=send_sem.at[phase],
            recv_sem=recv_sem.at[phase],
            device_id={"tp": peer},
            device_id_type=MESH,
        )

    def all_kv(phase, buffer):
        return to_kv(phase, buffer.at[pl.ds(0, KV - 1)], buffer.at[pl.ds(0, KV - 1)], kv)

    row = lax.broadcasted_iota(jnp.int32, (HD, HD), 0)
    column = lax.broadcasted_iota(jnp.int32, (HD, HD), 1)
    common = row & column
    parity = common
    for shift in (4, 2, 1):
        parity = parity ^ (parity >> shift)
    turn = ((1 - 2 * (parity & 1)).astype(f32) * (1.0 / HD)).astype(bf16)
    loads[0].wait()
    loads[1].wait()
    wide = queries[...].astype(f32)
    heads = jnp.concatenate(
        [wide[:, head * HD : (head + 1) * HD] for head in range(HEADS)], axis=0
    )
    sign = (1 - 2 * signs[...]).astype(f32)
    rotated[kv] = dot((heads * sign).astype(bf16), turn).astype(bf16)

    pl.semaphore_wait(barrier, KV + TP - 2)

    for peer in kv_peers:
        to_kv(0, rotated.at[kv], rotated.at[kv], peer).start()

    loads[9].wait()
    loads[10].wait()
    page_lane = lax.broadcasted_iota(jnp.int32, (1, 128), 1)
    owners = jnp.zeros((1, 128), jnp.int32)
    for request in range(KV):
        for slot in range(SLOTS):
            page = jnp.where(slot < count[0, request], table[0, slot, request], -1)
            owners = jnp.where(page_lane == page, request, owners)
    owner_row[...] = owners
    owner_copy = pltpu.make_async_copy(owner_row, owner, load_sem.at[11])
    owner_copy.start()
    gate[:, UNITS:] = jnp.zeros((FEATURES, PADDED - UNITS), bf16)
    up[:, UNITS:] = jnp.zeros((FEATURES, PADDED - UNITS), bf16)
    down[UNITS:, :] = jnp.zeros((TP * CHUNK - UNITS, FEATURES), bf16)

    loads[2].wait()
    loads[3].wait()
    for head in range(HEADS):
        stage[pl.ds(head, KV, stride=HEADS), :] = residual[:, head * HD : (head + 1) * HD].astype(
            f32
        )
    own_residual = stage[pl.ds(pl.multiple_of(kv * HEADS, HEADS), HEADS), :]

    owner_copy.wait()
    loads[4].wait()
    loads[5].wait()
    all_kv(0, rotated).wait_recv()

    pages = range(PAGES)
    scores = [
        lax.dot_general(
            rotated[owner[0, page]],
            keys[page],
            (((1,), (1,)), ((), ())),
            preferred_element_type=f32,
        )
        for page in pages
    ]
    largest = [jnp.max(score, axis=1, keepdims=True) for score in scores]
    weights = [jnp.exp(score - best).astype(bf16) for score, best in zip(scores, largest)]
    totals = [jnp.sum(weight.astype(f32), axis=1, keepdims=True) for weight in weights]
    for page in pages:
        page_max[page] = jnp.broadcast_to(largest[page], (HEADS, HD))
        page_total[page] = jnp.broadcast_to(totals[page], (HEADS, HD))

    lane = lax.broadcasted_iota(jnp.int32, (HEADS, 128), 1)
    levels = jnp.zeros((HEADS, 128), f32)
    owned = [[table[0, slot, request] for slot in range(SLOTS)] for request in range(KV)]
    shares = []
    for request in range(KV):
        live = count[0, request]
        tops = [
            jnp.where(slot < live, page_max[page], fill_value)
            for slot, page in enumerate(owned[request])
        ]
        best = jnp.maximum(jnp.maximum(tops[0], tops[1]), jnp.maximum(tops[2], tops[3]))
        factors = [jnp.exp(top - best) for top in tops]
        total = sum(factor * page_total[page] for factor, page in zip(factors, owned[request]))
        shares.append([factor / total for factor in factors])
        which, place = pair_of(request)
        for part, value in enumerate(split3(best + jnp.log(total))):
            levels = jnp.where(lane == part * KV + 2 * which + place, value, levels)
    level_out[...] = levels.astype(bf16)
    for peer in kv_peers:
        to_kv(7, level_out, level_in.at[kv], peer).start()
    level_in[kv] = level_out[...]

    outs = [dot(weight, values[page]) for page, weight in zip(pages, weights)]
    for page in pages:
        page_out[page] = outs[page]
    merged = [
        sum(share * page_out[page] for share, page in zip(shares[request], owned[request]))
        for request in range(KV)
    ]
    for request in range(KV):
        which, place = pair_of(request)
        part_out[which, place] = merged[request].astype(bf16)
    for peer in kv_peers:
        to_kv(1, part_out.at[pair_of(peer)[0]], part_in.at[kv], peer).start()
    part_in[kv] = part_out[pair]

    picked_lane = lax.broadcasted_iota(jnp.int32, (128, 2 * HD), 0)
    picked_column = lax.broadcasted_iota(jnp.int32, (128, 2 * HD), 1)
    pick = (
        (picked_lane < 3 * KV)
        & (lax.rem(picked_lane, KV) == 2 * pair + jnp.where(picked_column < HD, 0, 1))
    ).astype(f32).astype(bf16)
    all_kv(7, level_in).wait_recv()
    level = dot(level_in[...].reshape(KV * HEADS, 128), pick).reshape(KV, HEADS, 2 * HD)
    factor = jnp.exp(level - jnp.max(level, axis=0, keepdims=True))
    whole = jnp.sum(factor, axis=0)
    factor = factor / whole[None]
    all_kv(1, part_in).wait_recv()
    both = [
        jnp.sum(factor[:, :, place * HD : (place + 1) * HD] * part_in[:, place].astype(f32), axis=0)
        for place in range(2)
    ]
    for place in range(2):
        attended[pair, place] = both[place].astype(bf16)
    for peer in near_peers:
        to_kv(2, attended.at[pair], attended.at[pair], peer).start()
    attention = jnp.where(member == 0, both[0], both[1]).astype(bf16)
    own_stream = own_residual + attention.astype(f32)

    def near_kv(phase, buffer):
        return to_kv(phase, buffer.at[pl.ds(0, 7)], buffer.at[pl.ds(0, 7)], kv)

    near_kv(2, attended).wait_recv()
    for request in range(KV):
        which, place = pair_of(request)
        stage[request * HEADS : (request + 1) * HEADS, :] = attended[which, place].astype(f32)
    squares = jnp.zeros((KV, HD), f32)
    for head in range(HEADS):
        span = slice(head * HD, (head + 1) * HD)
        piece = residual[:, span].astype(f32) + stage[pl.ds(head, KV, stride=HEADS), :]
        squares = squares + piece * piece
        scaled[:, span] = (piece * gain[span].astype(f32)[None, :]).astype(bf16)
    square_out[...] = in_lanes(split3(jnp.sum(squares, axis=1, keepdims=True)))
    square_in[tp] = square_out[...]

    for peer in tp_peers:
        to_tp(3, square_out, square_in.at[tp], peer).start()

    loads[6].wait()
    loads[7].wait()

    for step, peer in enumerate(chunk_order):
        span = pl.ds(pl.multiple_of(peer * CHUNK, CHUNK), CHUNK)
        sums_out[peer, :, :CHUNK] = dot(scaled[...], gate[:, span]).astype(bf16)
        sums_out[peer, :, CHUNK:] = dot(scaled[...], up[:, span]).astype(bf16)
        if step < CHUNKS - 1:
            to_tp(4, sums_out.at[peer], sums_in.at[tp], peer).start()

    @pl.when(tp == CHUNKS)
    def _():
        to_tp(4, sums_out.at[CHUNKS - 1], sums_in.at[tp], CHUNKS - 1).start()

    def all_tp(phase, buffer, size):
        return to_tp(phase, buffer.at[pl.ds(0, size)], buffer.at[pl.ds(0, size)], tp)

    all_tp(3, square_in, TP - 1).wait_recv()
    mean = jnp.sum(jnp.sum(square_in[...].astype(f32), axis=0), axis=1, keepdims=True) / (
        FEATURES * TP
    )
    inverse = lax.rsqrt(mean + epsilon)

    def activate(gate_sum, up_sum):
        value = gate_sum * inverse
        return (value / (1.0 + jnp.exp(-value)) * (up_sum * inverse)).astype(bf16)

    @pl.when(tp < CHUNKS)
    def _():
        sums_in[tp] = sums_out[tp]
        all_tp(4, sums_in, TP - 1).wait_recv()
        total = jnp.sum(sums_in[...].astype(f32), axis=0)
        hidden[tp] = activate(total[:, :CHUNK], total[:, CHUNK:])

    @pl.when(tp == CHUNKS)
    def _():
        hidden[CHUNKS] = jnp.zeros((KV, CHUNK), bf16)

    for peer in tp_peers[:2]:
        to_tp(5, hidden.at[tp], hidden.at[tp], peer).start()
    for peer in tp_peers[2:6]:
        to_tp(8, hidden.at[tp], hidden.at[tp], peer).start()
    sibling = tp_peers[6]
    to_tp(9, hidden.at[tp], hidden.at[tp], sibling).start()

    def chip_product(chip):
        units = jnp.concatenate([hidden[2 * chip], hidden[2 * chip + 1]], axis=1)
        return dot(units, down[pl.ds(pl.multiple_of(chip * 2 * CHUNK, 2 * CHUNK), 2 * CHUNK), :])

    loads[8].wait()
    to_tp(9, hidden.at[sibling], hidden.at[sibling], sibling).wait_recv()
    product[...] = chip_product(y)
    all_tp(8, hidden, 4).wait_recv()
    product[...] += chip_product(lax.rem(y + 1, 4)) + chip_product(lax.rem(y + 3, 4))
    all_tp(5, hidden, 2).wait_recv()
    result = product[...] + chip_product(lax.rem(y + 2, 4))
    for head in range(HEADS):
        stage[pl.ds(head, KV, stride=HEADS), :] = result[:, head * HD : (head + 1) * HD]
    mixed_out[...] = stage[...].astype(bf16).reshape(KV, HEADS, HD)
    for peer in kv_peers:
        to_kv(6, mixed_out.at[peer], mixed_in.at[kv], peer).start()
    mixed_in[kv] = mixed_out[kv]
    all_kv(6, mixed_in).wait_recv()
    out[...] = (own_stream + jnp.sum(mixed_in[...].astype(f32), axis=0)).astype(bf16)

    all_kv(0, rotated).wait_send()
    all_kv(1, part_in).wait_send()
    near_kv(2, attended).wait_send()
    all_kv(7, level_in).wait_send()
    all_tp(3, square_in, TP - 1).wait_send()
    all_kv(6, mixed_out).wait_send()
    all_tp(5, hidden, 2).wait_send()
    all_tp(8, hidden, 4).wait_send()
    all_tp(9, hidden, 1).wait_send()

    @pl.when(tp < CHUNKS)
    def _():
        all_tp(4, sums_out, CHUNKS - 1).wait_send()

    @pl.when(tp == CHUNKS)
    def _():
        all_tp(4, sums_out, CHUNKS).wait_send()


def shards(
    queries,
    sign_bits,
    key_pages,
    value_pages,
    page_table,
    page_count,
    residual,
    norm_gain,
    gate_weight,
    up_weight,
    down_weight,
):
    in_hbm = pl.BlockSpec(memory_space=pltpu.HBM)
    result = pl.pallas_call(
        layer,
        out_shape=pltpu.VMEM((HEADS, HD), bf16),
        in_specs=[in_hbm] * 11,
        out_specs=pl.BlockSpec(memory_space=pltpu.VMEM),
        scratch_shapes=[
            pltpu.SMEM((1, SLOTS, KV), jnp.int32),
            pltpu.SMEM((1, KV), jnp.int32),
            pltpu.VMEM(queries.shape, bf16),
            pltpu.VMEM((1, HD), jnp.int32),
            pltpu.VMEM((1, 128), jnp.int32),
            pltpu.SMEM((1, 128), jnp.int32),
            pltpu.VMEM(key_pages.shape, bf16),
            pltpu.VMEM(value_pages.shape, bf16),
            pltpu.VMEM(residual.shape, bf16),
            pltpu.VMEM((FEATURES,), bf16),
            pltpu.VMEM((FEATURES, PADDED), bf16),
            pltpu.VMEM((FEATURES, PADDED), bf16),
            pltpu.VMEM((TP * CHUNK, FEATURES), bf16),
            pltpu.VMEM((KV, HEADS, HD), bf16),
            pltpu.VMEM((PAGES, HEADS, HD), f32),
            pltpu.VMEM((PAGES, HEADS, HD), f32),
            pltpu.VMEM((PAGES, HEADS, HD), f32),
            pltpu.VMEM((HEADS, 128), bf16),
            pltpu.VMEM((KV, HEADS, 128), bf16),
            pltpu.VMEM((KV // 2, 2, HEADS, HD), bf16),
            pltpu.VMEM((KV, 2, HEADS, HD), bf16),
            pltpu.VMEM((KV // 2, 2, HEADS, HD), bf16),
            pltpu.VMEM((KV * HEADS, HD), f32),
            pltpu.VMEM((KV, FEATURES), bf16),
            pltpu.VMEM((KV, 128), bf16),
            pltpu.VMEM((TP, KV, 128), bf16),
            pltpu.VMEM((CHUNKS, KV, 2 * CHUNK), bf16),
            pltpu.VMEM((TP, KV, 2 * CHUNK), bf16),
            pltpu.VMEM((TP, KV, CHUNK), bf16),
            pltpu.VMEM((KV, FEATURES), f32),
            pltpu.VMEM((KV, HEADS, HD), bf16),
            pltpu.VMEM((KV, HEADS, HD), bf16),
            pltpu.SemaphoreType.DMA((12,)),
            pltpu.SemaphoreType.DMA((10,)),
            pltpu.SemaphoreType.DMA((10,)),
        ],
        compiler_params=pltpu.CompilerParams(
            collective_id=0, has_side_effects=True, vmem_limit_bytes=63 * 1024 * 1024
        ),
    )(
        jnp.transpose(page_table, (0, 2, 1)),
        page_count,
        queries,
        sign_bits.reshape(1, HD),
        key_pages,
        value_pages,
        residual,
        norm_gain,
        gate_weight,
        up_weight,
        down_weight,
    )
    return result.reshape(1, FEATURES)


def solution(mesh):
    in_specs = (
        P("kv", "tp"),
        P(),
        P("kv", None, "tp"),
        P("kv", None, "tp"),
        P("kv", None, None),
        P("kv", None),
        P(None, "tp"),
        P("tp"),
        P("tp", "kv"),
        P("tp", "kv"),
        P("kv", "tp"),
    )
    out_specs = P("kv", "tp")
    return jax.shard_map(shards, mesh=mesh, in_specs=in_specs, out_specs=out_specs, check_vma=False)
```

```python
from functools import partial

import jax
import jax.numpy as jnp
from jax import lax
from jax.experimental import pallas as pl
from jax.experimental.pallas import tpu as pltpu
from jax.sharding import PartitionSpec as P

fill_value = -1e30
epsilon = 1e-05
f32 = jnp.float32
bf16 = jnp.bfloat16
MESH = pl.DeviceIdType.MESH

KV = 16
TP = 8
HEADS = 16
HD = 128
SLOTS = 4
PAGES = 32
FEATURES = HEADS * HD
UNITS = 1664
CHUNK = 256
CHUNKS = -(-UNITS // CHUNK)
PADDED = CHUNKS * CHUNK


def dot(left, right):
    return jnp.dot(left, right, preferred_element_type=f32)


def pair_of(kv):
    x, z = kv // 4, kv % 4
    return (x % 2) * 4 + (z + 2 * (x // 2)) % 4, x // 2


def split3(value):
    high = value.astype(bf16).astype(f32)
    rest = value - high
    middle = rest.astype(bf16).astype(f32)
    return high, middle, rest - middle


def in_lanes(parts):
    rows = parts[0].shape[0]
    lane = lax.broadcasted_iota(jnp.int32, (rows, 128), 1)
    tile = jnp.zeros((rows, 128), f32)
    for place, part in enumerate(parts):
        tile = jnp.where(lane == place, part, tile)
    return tile.astype(bf16)


def layer(
    table_hbm,
    count_hbm,
    queries_hbm,
    signs_hbm,
    keys_hbm,
    values_hbm,
    residual_hbm,
    gain_hbm,
    gate_hbm,
    up_hbm,
    down_hbm,
    out,
    table,
    count,
    queries,
    signs,
    owner_row,
    owner,
    keys,
    values,
    residual,
    gain,
    gate,
    up,
    down,
    rotated,
    page_max,
    page_total,
    page_out,
    part_out,
    part_in,
    attended,
    stage,
    scaled,
    square_out,
    square_in,
    sums_out,
    sums_in,
    hidden,
    product,
    mixed_out,
    mixed_in,
    load_sem,
    send_sem,
    recv_sem,
):
    kv = lax.axis_index("kv")
    tp = lax.axis_index("tp")

    loads = [
        pltpu.make_async_copy(source, target, load_sem.at[place])
        for place, (source, target) in enumerate(
            [
                (queries_hbm, queries),
                (signs_hbm, signs),
                (residual_hbm, residual),
                (gain_hbm, gain),
                (keys_hbm, keys),
                (values_hbm, values),
                (gate_hbm, gate.at[:, pl.ds(0, UNITS)]),
                (up_hbm, up.at[:, pl.ds(0, UNITS)]),
                (down_hbm, down.at[pl.ds(0, UNITS)]),
                (table_hbm, table),
                (count_hbm, count),
            ]
        )
    ]
    loads[0].start()
    loads[1].start()

    x, z = kv // 4, lax.rem(kv, 4)
    offsets = [(dx, dz) for dx in range(4) for dz in range(4) if dx or dz]
    offsets.sort(key=lambda at: -min(at[0], 4 - at[0]) - min(at[1], 4 - at[1]))
    kv_peers = [lax.rem(x + dx, 4) * 4 + lax.rem(z + dz, 4) for dx, dz in offsets]
    pair, member = pair_of(kv)
    near = [(0, 2), (1, 1), (3, 1), (0, 1), (0, 3), (1, 0), (3, 0)]
    near_peers = [lax.rem(x + dx, 4) * 4 + lax.rem(z + dz, 4) for dx, dz in near]

    y, core = tp // 2, tp % 2
    row = [
        lax.rem(y + dy, 4) * 2 + side
        for dy in (2, 1, 3, 0)
        for side in ((core, 1 - core) if dy else (1 - core, core))
    ]
    tp_peers = row[:-1]
    gap = sum(jnp.where(peer == TP - 1, place, 0) for place, peer in enumerate(row))
    chunk_order = [
        jnp.where(place < gap, row[place], row[place + 1]) for place in range(CHUNKS)
    ]

    barrier = pltpu.get_barrier_semaphore()
    for peer in kv_peers:
        pl.semaphore_signal(barrier, inc=1, device_id={"kv": peer}, device_id_type=MESH)
    for peer in tp_peers:
        pl.semaphore_signal(barrier, inc=1, device_id={"tp": peer}, device_id_type=MESH)

    for place in (9, 10, 2, 3, 4, 5, 6, 7, 8):
        loads[place].start()

    def to_kv(phase, source, target, peer):
        return pltpu.make_async_remote_copy(
            src_ref=source,
            dst_ref=target,
            send_sem=send_sem.at[phase],
            recv_sem=recv_sem.at[phase],
            device_id={"kv": peer},
            device_id_type=MESH,
        )

    def to_tp(phase, source, target, peer):
        return pltpu.make_async_remote_copy(
            src_ref=source,
            dst_ref=target,
            send_sem=send_sem.at[phase],
            recv_sem=recv_sem.at[phase],
            device_id={"tp": peer},
            device_id_type=MESH,
        )

    def all_kv(phase, buffer):
        return to_kv(phase, buffer.at[pl.ds(0, KV - 1)], buffer.at[pl.ds(0, KV - 1)], kv)

    row = lax.broadcasted_iota(jnp.int32, (HD, HD), 0)
    column = lax.broadcasted_iota(jnp.int32, (HD, HD), 1)
    common = row & column
    parity = common
    for shift in (4, 2, 1):
        parity = parity ^ (parity >> shift)
    turn = ((1 - 2 * (parity & 1)).astype(f32) * (1.0 / HD)).astype(bf16)
    loads[0].wait()
    loads[1].wait()
    wide = queries[...].astype(f32)
    heads = jnp.concatenate(
        [wide[:, head * HD : (head + 1) * HD] for head in range(HEADS)], axis=0
    )
    sign = (1 - 2 * signs[...]).astype(f32)
    rotated[kv] = dot((heads * sign).astype(bf16), turn).astype(bf16)

    pl.semaphore_wait(barrier, KV + TP - 2)

    for peer in kv_peers:
        to_kv(0, rotated.at[kv], rotated.at[kv], peer).start()

    loads[9].wait()
    loads[10].wait()
    page_lane = lax.broadcasted_iota(jnp.int32, (1, 128), 1)
    owners = jnp.zeros((1, 128), jnp.int32)
    for request in range(KV):
        for slot in range(SLOTS):
            page = jnp.where(slot < count[0, request], table[0, slot, request], -1)
            owners = jnp.where(page_lane == page, request, owners)
    owner_row[...] = owners
    owner_copy = pltpu.make_async_copy(owner_row, owner, load_sem.at[11])
    owner_copy.start()
    gate[:, UNITS:] = jnp.zeros((FEATURES, PADDED - UNITS), bf16)
    up[:, UNITS:] = jnp.zeros((FEATURES, PADDED - UNITS), bf16)
    down[UNITS:, :] = jnp.zeros((TP * CHUNK - UNITS, FEATURES), bf16)

    loads[2].wait()
    loads[3].wait()
    for head in range(HEADS):
        stage[pl.ds(head, KV, stride=HEADS), :] = residual[:, head * HD : (head + 1) * HD].astype(
            f32
        )
    own_residual = stage[pl.ds(pl.multiple_of(kv * HEADS, HEADS), HEADS), :]

    owner_copy.wait()
    loads[4].wait()
    loads[5].wait()
    all_kv(0, rotated).wait_recv()

    pages = range(PAGES)
    scores = [
        lax.dot_general(
            rotated[owner[0, page]],
            keys[page],
            (((1,), (1,)), ((), ())),
            preferred_element_type=f32,
        )
        for page in pages
    ]
    largest = [jnp.max(score, axis=1, keepdims=True) for score in scores]
    weights = [jnp.exp(score - best).astype(bf16) for score, best in zip(scores, largest)]
    totals = [jnp.sum(weight.astype(f32), axis=1, keepdims=True) for weight in weights]
    for page in pages:
        page_max[page] = jnp.broadcast_to(largest[page], (HEADS, HD))
        page_total[page] = jnp.broadcast_to(totals[page], (HEADS, HD))

    lane = lax.broadcasted_iota(jnp.int32, (HEADS, 128), 1)
    levels = jnp.zeros((HEADS, 128), f32)
    owned = [[table[0, slot, request] for slot in range(SLOTS)] for request in range(KV)]
    shares = []
    for request in range(KV):
        live = count[0, request]
        tops = [
            jnp.where(slot < live, page_max[page], fill_value)
            for slot, page in enumerate(owned[request])
        ]
        best = jnp.maximum(jnp.maximum(tops[0], tops[1]), jnp.maximum(tops[2], tops[3]))
        factors = [jnp.exp(top - best) for top in tops]
        total = sum(factor * page_total[page] for factor, page in zip(factors, owned[request]))
        shares.append([factor / total for factor in factors])
        which, place = pair_of(request)
        for part, value in enumerate(split3(best + jnp.log(total))):
            levels = jnp.where(lane == part * KV + 2 * which + place, value, levels)
    level_tile = levels.astype(bf16)
    for which in range(KV // 2):
        part_out[which, 2] = level_tile
    outs = [dot(weight, values[page]) for page, weight in zip(pages, weights)]
    for page in pages:
        page_out[page] = outs[page]
    merged = [
        sum(share * page_out[page] for share, page in zip(shares[request], owned[request]))
        for request in range(KV)
    ]
    for request in range(KV):
        which, place = pair_of(request)
        part_out[which, place] = merged[request].astype(bf16)
    for peer in kv_peers:
        to_kv(1, part_out.at[pair_of(peer)[0]], part_in.at[kv], peer).start()
    part_in[kv] = part_out[pair]

    picked_lane = lax.broadcasted_iota(jnp.int32, (128, 2 * HD), 0)
    picked_column = lax.broadcasted_iota(jnp.int32, (128, 2 * HD), 1)
    pick = (
        (picked_lane < 3 * KV)
        & (lax.rem(picked_lane, KV) == 2 * pair + jnp.where(picked_column < HD, 0, 1))
    ).astype(f32).astype(bf16)
    all_kv(1, part_in).wait_recv()
    level = dot(part_in[:, 2].reshape(KV * HEADS, 128), pick).reshape(KV, HEADS, 2 * HD)
    factor = jnp.exp(level - jnp.max(level, axis=0, keepdims=True))
    whole = jnp.sum(factor, axis=0)
    factor = factor / whole[None]
    both = [
        jnp.sum(factor[:, :, place * HD : (place + 1) * HD] * part_in[:, place].astype(f32), axis=0)
        for place in range(2)
    ]
    for place in range(2):
        attended[pair, place] = both[place].astype(bf16)
    for peer in near_peers:
        to_kv(2, attended.at[pair], attended.at[pair], peer).start()
    attention = jnp.where(member == 0, both[0], both[1]).astype(bf16)
    own_stream = own_residual + attention.astype(f32)

    def near_kv(phase, buffer):
        return to_kv(phase, buffer.at[pl.ds(0, 7)], buffer.at[pl.ds(0, 7)], kv)

    near_kv(2, attended).wait_recv()
    for request in range(KV):
        which, place = pair_of(request)
        stage[request * HEADS : (request + 1) * HEADS, :] = attended[which, place].astype(f32)
    squares = jnp.zeros((KV, HD), f32)
    for head in range(HEADS):
        span = slice(head * HD, (head + 1) * HD)
        piece = residual[:, span].astype(f32) + stage[pl.ds(head, KV, stride=HEADS), :]
        squares = squares + piece * piece
        scaled[:, span] = (piece * gain[span].astype(f32)[None, :]).astype(bf16)
    square_out[...] = in_lanes(split3(jnp.sum(squares, axis=1, keepdims=True)))
    square_in[tp] = square_out[...]

    loads[6].wait()
    loads[7].wait()

    for step, peer in enumerate(chunk_order):
        span = pl.ds(pl.multiple_of(peer * CHUNK, CHUNK), CHUNK)
        sums_out[peer, :, :CHUNK] = dot(scaled[...], gate[:, span]).astype(bf16)
        sums_out[peer, :, CHUNK:] = dot(scaled[...], up[:, span]).astype(bf16)
        if step < CHUNKS - 1:
            to_tp(4, sums_out.at[peer], sums_in.at[tp], peer).start()
        if step == 1:
            for target in tp_peers:
                to_tp(3, square_out, square_in.at[tp], target).start()

    @pl.when(tp == CHUNKS)
    def _():
        to_tp(4, sums_out.at[CHUNKS - 1], sums_in.at[tp], CHUNKS - 1).start()

    def all_tp(phase, buffer, size):
        return to_tp(phase, buffer.at[pl.ds(0, size)], buffer.at[pl.ds(0, size)], tp)

    all_tp(3, square_in, TP - 1).wait_recv()
    mean = jnp.sum(jnp.sum(square_in[...].astype(f32), axis=0), axis=1, keepdims=True) / (
        FEATURES * TP
    )
    inverse = lax.rsqrt(mean + epsilon)

    def activate(gate_sum, up_sum):
        value = gate_sum * inverse
        return (value / (1.0 + jnp.exp(-value)) * (up_sum * inverse)).astype(bf16)

    @pl.when(tp < CHUNKS)
    def _():
        sums_in[tp] = sums_out[tp]
        all_tp(4, sums_in, TP - 1).wait_recv()
        total = jnp.sum(sums_in[...].astype(f32), axis=0)
        hidden[tp] = activate(total[:, :CHUNK], total[:, CHUNK:])

    @pl.when(tp == CHUNKS)
    def _():
        hidden[CHUNKS] = jnp.zeros((KV, CHUNK), bf16)

    for peer in tp_peers[:2]:
        to_tp(5, hidden.at[tp], hidden.at[tp], peer).start()
    for peer in tp_peers[2:6]:
        to_tp(8, hidden.at[tp], hidden.at[tp], peer).start()
    sibling = tp_peers[6]
    to_tp(9, hidden.at[tp], hidden.at[tp], sibling).start()

    def chip_product(chip):
        units = jnp.concatenate([hidden[2 * chip], hidden[2 * chip + 1]], axis=1)
        return dot(units, down[pl.ds(pl.multiple_of(chip * 2 * CHUNK, 2 * CHUNK), 2 * CHUNK), :])

    loads[8].wait()
    to_tp(9, hidden.at[sibling], hidden.at[sibling], sibling).wait_recv()
    product[...] = chip_product(y)
    all_tp(8, hidden, 4).wait_recv()
    product[...] += chip_product(lax.rem(y + 1, 4)) + chip_product(lax.rem(y + 3, 4))
    all_tp(5, hidden, 2).wait_recv()
    result = product[...] + chip_product(lax.rem(y + 2, 4))
    for head in range(HEADS):
        stage[pl.ds(head, KV, stride=HEADS), :] = result[:, head * HD : (head + 1) * HD]
    mixed_out[...] = stage[...].astype(bf16).reshape(KV, HEADS, HD)
    for peer in kv_peers:
        to_kv(6, mixed_out.at[peer], mixed_in.at[kv], peer).start()
    mixed_in[kv] = mixed_out[kv]
    all_kv(6, mixed_in).wait_recv()
    out[...] = (own_stream + jnp.sum(mixed_in[...].astype(f32), axis=0)).astype(bf16)

    all_kv(0, rotated).wait_send()
    all_kv(1, part_in).wait_send()
    near_kv(2, attended).wait_send()
    all_tp(3, square_in, TP - 1).wait_send()
    all_kv(6, mixed_out).wait_send()
    all_tp(5, hidden, 2).wait_send()
    all_tp(8, hidden, 4).wait_send()
    all_tp(9, hidden, 1).wait_send()

    @pl.when(tp < CHUNKS)
    def _():
        all_tp(4, sums_out, CHUNKS - 1).wait_send()

    @pl.when(tp == CHUNKS)
    def _():
        all_tp(4, sums_out, CHUNKS).wait_send()


def shards(
    queries,
    sign_bits,
    key_pages,
    value_pages,
    page_table,
    page_count,
    residual,
    norm_gain,
    gate_weight,
    up_weight,
    down_weight,
):
    in_hbm = pl.BlockSpec(memory_space=pltpu.HBM)
    result = pl.pallas_call(
        layer,
        out_shape=pltpu.VMEM((HEADS, HD), bf16),
        in_specs=[in_hbm] * 11,
        out_specs=pl.BlockSpec(memory_space=pltpu.VMEM),
        scratch_shapes=[
            pltpu.SMEM((1, SLOTS, KV), jnp.int32),
            pltpu.SMEM((1, KV), jnp.int32),
            pltpu.VMEM(queries.shape, bf16),
            pltpu.VMEM((1, HD), jnp.int32),
            pltpu.VMEM((1, 128), jnp.int32),
            pltpu.SMEM((1, 128), jnp.int32),
            pltpu.VMEM(key_pages.shape, bf16),
            pltpu.VMEM(value_pages.shape, bf16),
            pltpu.VMEM(residual.shape, bf16),
            pltpu.VMEM((FEATURES,), bf16),
            pltpu.VMEM((FEATURES, PADDED), bf16),
            pltpu.VMEM((FEATURES, PADDED), bf16),
            pltpu.VMEM((TP * CHUNK, FEATURES), bf16),
            pltpu.VMEM((KV, HEADS, HD), bf16),
            pltpu.VMEM((PAGES, HEADS, HD), f32),
            pltpu.VMEM((PAGES, HEADS, HD), f32),
            pltpu.VMEM((PAGES, HEADS, HD), f32),
            pltpu.VMEM((KV // 2, 3, HEADS, HD), bf16),
            pltpu.VMEM((KV, 3, HEADS, HD), bf16),
            pltpu.VMEM((KV // 2, 2, HEADS, HD), bf16),
            pltpu.VMEM((KV * HEADS, HD), f32),
            pltpu.VMEM((KV, FEATURES), bf16),
            pltpu.VMEM((KV, 128), bf16),
            pltpu.VMEM((TP, KV, 128), bf16),
            pltpu.VMEM((CHUNKS, KV, 2 * CHUNK), bf16),
            pltpu.VMEM((TP, KV, 2 * CHUNK), bf16),
            pltpu.VMEM((TP, KV, CHUNK), bf16),
            pltpu.VMEM((KV, FEATURES), f32),
            pltpu.VMEM((KV, HEADS, HD), bf16),
            pltpu.VMEM((KV, HEADS, HD), bf16),
            pltpu.SemaphoreType.DMA((12,)),
            pltpu.SemaphoreType.DMA((10,)),
            pltpu.SemaphoreType.DMA((10,)),
        ],
        compiler_params=pltpu.CompilerParams(
            collective_id=0, has_side_effects=True, vmem_limit_bytes=63 * 1024 * 1024
        ),
    )(
        jnp.transpose(page_table, (0, 2, 1)),
        page_count,
        queries,
        sign_bits.reshape(1, HD),
        key_pages,
        value_pages,
        residual,
        norm_gain,
        gate_weight,
        up_weight,
        down_weight,
    )
    return result.reshape(1, FEATURES)


def solution(mesh):
    in_specs = (
        P("kv", "tp"),
        P(),
        P("kv", None, "tp"),
        P("kv", None, "tp"),
        P("kv", None, None),
        P("kv", None),
        P(None, "tp"),
        P("tp"),
        P("tp", "kv"),
        P("tp", "kv"),
        P("kv", "tp"),
    )
    out_specs = P("kv", "tp")
    return jax.shard_map(shards, mesh=mesh, in_specs=in_specs, out_specs=out_specs, check_vma=False)
```

```python
from functools import partial

import jax
import jax.numpy as jnp
from jax import lax
from jax.experimental import pallas as pl
from jax.experimental.pallas import tpu as pltpu
from jax.sharding import PartitionSpec as P

fill_value = -1e30
epsilon = 1e-05
f32 = jnp.float32
bf16 = jnp.bfloat16
MESH = pl.DeviceIdType.MESH

KV = 16
TP = 8
HEADS = 16
HD = 128
SLOTS = 4
PAGES = 32
FEATURES = HEADS * HD
UNITS = 1664
CHUNK = 256
CHUNKS = -(-UNITS // CHUNK)
PADDED = CHUNKS * CHUNK


def dot(left, right):
    return jnp.dot(left, right, preferred_element_type=f32)


def pair_of(kv):
    x, z = kv // 4, kv % 4
    return (x % 2) * 4 + (z + 2 * (x // 2)) % 4, x // 2


def split3(value):
    high = value.astype(bf16).astype(f32)
    rest = value - high
    middle = rest.astype(bf16).astype(f32)
    return high, middle, rest - middle


def in_lanes(parts):
    rows = parts[0].shape[0]
    lane = lax.broadcasted_iota(jnp.int32, (rows, 128), 1)
    tile = jnp.zeros((rows, 128), f32)
    for place, part in enumerate(parts):
        tile = jnp.where(lane == place, part, tile)
    return tile.astype(bf16)


def layer(
    table_hbm,
    count_hbm,
    queries_hbm,
    signs_hbm,
    keys_hbm,
    values_hbm,
    residual_hbm,
    gain_hbm,
    gate_hbm,
    up_hbm,
    down_hbm,
    out,
    table,
    count,
    queries,
    signs,
    owner_row,
    owner,
    keys,
    values,
    residual,
    gain,
    gate,
    up,
    down,
    rotated,
    page_max,
    page_total,
    page_out,
    part_out,
    part_in,
    attended,
    stage,
    scaled,
    square_out,
    square_in,
    sums_out,
    sums_in,
    hidden,
    product,
    mixed_out,
    mixed_in,
    load_sem,
    send_sem,
    recv_sem,
):
    kv = lax.axis_index("kv")
    tp = lax.axis_index("tp")

    loads = [
        pltpu.make_async_copy(source, target, load_sem.at[place])
        for place, (source, target) in enumerate(
            [
                (queries_hbm, queries),
                (signs_hbm, signs),
                (residual_hbm, residual),
                (gain_hbm, gain),
                (keys_hbm, keys),
                (values_hbm, values),
                (gate_hbm, gate.at[:, pl.ds(0, UNITS)]),
                (up_hbm, up.at[:, pl.ds(0, UNITS)]),
                (down_hbm, down.at[pl.ds(0, UNITS)]),
                (table_hbm, table),
                (count_hbm, count),
            ]
        )
    ]
    loads[0].start()
    loads[1].start()

    x, z = kv // 4, lax.rem(kv, 4)
    offsets = [(dx, dz) for dx in range(4) for dz in range(4) if dx or dz]
    offsets.sort(key=lambda at: -min(at[0], 4 - at[0]) - min(at[1], 4 - at[1]))
    kv_peers = [lax.rem(x + dx, 4) * 4 + lax.rem(z + dz, 4) for dx, dz in offsets]
    pair, member = pair_of(kv)
    near = [(0, 2), (1, 1), (3, 1), (0, 1), (0, 3), (1, 0), (3, 0)]
    near_peers = [lax.rem(x + dx, 4) * 4 + lax.rem(z + dz, 4) for dx, dz in near]

    y, core = tp // 2, tp % 2
    row = [
        lax.rem(y + dy, 4) * 2 + side
        for dy in (2, 3, 1, 0)
        for side in ((core, 1 - core) if dy else (1 - core, core))
    ]
    tp_peers = row[:-1]
    gap = sum(jnp.where(peer == TP - 1, place, 0) for place, peer in enumerate(row))
    chunk_order = [
        jnp.where(place < gap, row[place], row[place + 1]) for place in range(CHUNKS)
    ]

    barrier = pltpu.get_barrier_semaphore()
    for peer in kv_peers:
        pl.semaphore_signal(barrier, inc=1, device_id={"kv": peer}, device_id_type=MESH)
    for peer in tp_peers:
        pl.semaphore_signal(barrier, inc=1, device_id={"tp": peer}, device_id_type=MESH)

    for place in (9, 10, 2, 3, 4, 5, 6, 7, 8):
        loads[place].start()

    def to_kv(phase, source, target, peer):
        return pltpu.make_async_remote_copy(
            src_ref=source,
            dst_ref=target,
            send_sem=send_sem.at[phase],
            recv_sem=recv_sem.at[phase],
            device_id={"kv": peer},
            device_id_type=MESH,
        )

    def to_tp(phase, source, target, peer):
        return pltpu.make_async_remote_copy(
            src_ref=source,
            dst_ref=target,
            send_sem=send_sem.at[phase],
            recv_sem=recv_sem.at[phase],
            device_id={"tp": peer},
            device_id_type=MESH,
        )

    def all_kv(phase, buffer):
        return to_kv(phase, buffer.at[pl.ds(0, KV - 1)], buffer.at[pl.ds(0, KV - 1)], kv)

    row = lax.broadcasted_iota(jnp.int32, (HD, HD), 0)
    column = lax.broadcasted_iota(jnp.int32, (HD, HD), 1)
    common = row & column
    parity = common
    for shift in (4, 2, 1):
        parity = parity ^ (parity >> shift)
    turn = ((1 - 2 * (parity & 1)).astype(f32) * (1.0 / HD)).astype(bf16)
    loads[0].wait()
    loads[1].wait()
    wide = queries[...].astype(f32)
    heads = jnp.concatenate(
        [wide[:, head * HD : (head + 1) * HD] for head in range(HEADS)], axis=0
    )
    sign = (1 - 2 * signs[...]).astype(f32)
    rotated[kv] = dot((heads * sign).astype(bf16), turn).astype(bf16)

    pl.semaphore_wait(barrier, KV + TP - 2)

    for peer in kv_peers:
        to_kv(0, rotated.at[kv], rotated.at[kv], peer).start()

    loads[9].wait()
    loads[10].wait()
    page_lane = lax.broadcasted_iota(jnp.int32, (1, 128), 1)
    owners = jnp.zeros((1, 128), jnp.int32)
    for request in range(KV):
        for slot in range(SLOTS):
            page = jnp.where(slot < count[0, request], table[0, slot, request], -1)
            owners = jnp.where(page_lane == page, request, owners)
    owner_row[...] = owners
    owner_copy = pltpu.make_async_copy(owner_row, owner, load_sem.at[11])
    owner_copy.start()
    gate[:, UNITS:] = jnp.zeros((FEATURES, PADDED - UNITS), bf16)
    up[:, UNITS:] = jnp.zeros((FEATURES, PADDED - UNITS), bf16)
    down[UNITS:, :] = jnp.zeros((TP * CHUNK - UNITS, FEATURES), bf16)

    loads[2].wait()
    loads[3].wait()
    for head in range(HEADS):
        stage[pl.ds(head, KV, stride=HEADS), :] = residual[:, head * HD : (head + 1) * HD].astype(
            f32
        )
    own_residual = stage[pl.ds(pl.multiple_of(kv * HEADS, HEADS), HEADS), :]

    owner_copy.wait()
    loads[4].wait()
    loads[5].wait()
    all_kv(0, rotated).wait_recv()

    pages = range(PAGES)
    scores = [
        lax.dot_general(
            rotated[owner[0, page]],
            keys[page],
            (((1,), (1,)), ((), ())),
            preferred_element_type=f32,
        )
        for page in pages
    ]
    largest = [jnp.max(score, axis=1, keepdims=True) for score in scores]
    weights = [jnp.exp(score - best).astype(bf16) for score, best in zip(scores, largest)]
    totals = [jnp.sum(weight.astype(f32), axis=1, keepdims=True) for weight in weights]
    for page in pages:
        page_max[page] = jnp.broadcast_to(largest[page], (HEADS, HD))
        page_total[page] = jnp.broadcast_to(totals[page], (HEADS, HD))

    lane = lax.broadcasted_iota(jnp.int32, (HEADS, 128), 1)
    levels = jnp.zeros((HEADS, 128), f32)
    owned = [[table[0, slot, request] for slot in range(SLOTS)] for request in range(KV)]
    shares = []
    for request in range(KV):
        live = count[0, request]
        tops = [
            jnp.where(slot < live, page_max[page], fill_value)
            for slot, page in enumerate(owned[request])
        ]
        best = jnp.maximum(jnp.maximum(tops[0], tops[1]), jnp.maximum(tops[2], tops[3]))
        factors = [jnp.exp(top - best) for top in tops]
        total = sum(factor * page_total[page] for factor, page in zip(factors, owned[request]))
        inverse_total = 1.0 / total
        shares.append([factor * inverse_total for factor in factors])
        which, place = pair_of(request)
        for part, value in enumerate(split3(best + jnp.log(total))):
            levels = jnp.where(lane == part * KV + 2 * which + place, value, levels)
    level_tile = levels.astype(bf16)
    for which in range(KV // 2):
        part_out[which, 2] = level_tile
    outs = [dot(weight, values[page]) for page, weight in zip(pages, weights)]
    for page in pages:
        page_out[page] = outs[page]
    merged = [
        sum(share * page_out[page] for share, page in zip(shares[request], owned[request]))
        for request in range(KV)
    ]
    for request in range(KV):
        which, place = pair_of(request)
        part_out[which, place] = merged[request].astype(bf16)
    for peer in kv_peers:
        to_kv(1, part_out.at[pair_of(peer)[0]], part_in.at[kv], peer).start()
    part_in[kv] = part_out[pair]

    picked_lane = lax.broadcasted_iota(jnp.int32, (128, 2 * HD), 0)
    picked_column = lax.broadcasted_iota(jnp.int32, (128, 2 * HD), 1)
    pick = (
        (picked_lane < 3 * KV)
        & (lax.rem(picked_lane, KV) == 2 * pair + jnp.where(picked_column < HD, 0, 1))
    ).astype(f32).astype(bf16)
    all_kv(1, part_in).wait_recv()
    level = dot(part_in[:, 2].reshape(KV * HEADS, 128), pick).reshape(KV, HEADS, 2 * HD)
    factor = jnp.exp(level - jnp.max(level, axis=0, keepdims=True))
    whole = jnp.sum(factor, axis=0)
    inverse_whole = 1.0 / whole
    both = [
        jnp.sum(factor[:, :, place * HD : (place + 1) * HD] * part_in[:, place].astype(f32), axis=0)
        * inverse_whole[:, place * HD : (place + 1) * HD]
        for place in range(2)
    ]
    for place in range(2):
        attended[pair, place] = both[place].astype(bf16)
    for peer in near_peers:
        to_kv(2, attended.at[pair], attended.at[pair], peer).start()
    attention = jnp.where(member == 0, both[0], both[1]).astype(bf16)
    own_stream = own_residual + attention.astype(f32)

    def near_kv(phase, buffer):
        return to_kv(phase, buffer.at[pl.ds(0, 7)], buffer.at[pl.ds(0, 7)], kv)

    near_kv(2, attended).wait_recv()
    for request in range(KV):
        which, place = pair_of(request)
        stage[request * HEADS : (request + 1) * HEADS, :] = attended[which, place].astype(f32)
    squares = jnp.zeros((KV, HD), f32)
    for head in range(HEADS):
        span = slice(head * HD, (head + 1) * HD)
        piece = residual[:, span].astype(f32) + stage[pl.ds(head, KV, stride=HEADS), :]
        squares = squares + piece * piece
        scaled[:, span] = (piece * gain[span].astype(f32)[None, :]).astype(bf16)
    square_out[...] = in_lanes(split3(jnp.sum(squares, axis=1, keepdims=True)))
    square_in[tp] = square_out[...]

    loads[6].wait()
    loads[7].wait()

    for step, peer in enumerate(chunk_order):
        span = pl.ds(pl.multiple_of(peer * CHUNK, CHUNK), CHUNK)
        sums_out[peer, :, :CHUNK] = dot(scaled[...], gate[:, span]).astype(bf16)
        sums_out[peer, :, CHUNK:] = dot(scaled[...], up[:, span]).astype(bf16)
        if step < CHUNKS - 1:
            to_tp(4, sums_out.at[peer], sums_in.at[tp], peer).start()
        if step == 1:
            for target in tp_peers:
                to_tp(3, square_out, square_in.at[tp], target).start()

    @pl.when(tp == CHUNKS)
    def _():
        to_tp(4, sums_out.at[CHUNKS - 1], sums_in.at[tp], CHUNKS - 1).start()

    def all_tp(phase, buffer, size):
        return to_tp(phase, buffer.at[pl.ds(0, size)], buffer.at[pl.ds(0, size)], tp)

    all_tp(3, square_in, TP - 1).wait_recv()
    mean = jnp.sum(jnp.sum(square_in[...].astype(f32), axis=0), axis=1, keepdims=True) / (
        FEATURES * TP
    )
    inverse = lax.rsqrt(mean + epsilon)

    def activate(gate_sum, up_sum):
        value = gate_sum * inverse
        return (value / (1.0 + jnp.exp(-value)) * (up_sum * inverse)).astype(bf16)

    @pl.when(tp < CHUNKS)
    def _():
        sums_in[tp] = sums_out[tp]
        all_tp(4, sums_in, TP - 1).wait_recv()
        total = jnp.sum(sums_in[...].astype(f32), axis=0)
        hidden[tp] = activate(total[:, :CHUNK], total[:, CHUNK:])

    @pl.when(tp == CHUNKS)
    def _():
        hidden[CHUNKS] = jnp.zeros((KV, CHUNK), bf16)

    for peer in tp_peers[:2]:
        to_tp(5, hidden.at[tp], hidden.at[tp], peer).start()
    for peer in tp_peers[2:6]:
        to_tp(8, hidden.at[tp], hidden.at[tp], peer).start()
    sibling = tp_peers[6]
    to_tp(9, hidden.at[tp], hidden.at[tp], sibling).start()

    def chip_product(chip):
        units = jnp.concatenate([hidden[2 * chip], hidden[2 * chip + 1]], axis=1)
        return dot(units, down[pl.ds(pl.multiple_of(chip * 2 * CHUNK, 2 * CHUNK), 2 * CHUNK), :])

    loads[8].wait()
    to_tp(9, hidden.at[sibling], hidden.at[sibling], sibling).wait_recv()
    product[...] = chip_product(y)
    all_tp(8, hidden, 4).wait_recv()
    product[...] += chip_product(lax.rem(y + 1, 4)) + chip_product(lax.rem(y + 3, 4))
    all_tp(5, hidden, 2).wait_recv()
    result = product[...] + chip_product(lax.rem(y + 2, 4))
    for head in range(HEADS):
        stage[pl.ds(head, KV, stride=HEADS), :] = result[:, head * HD : (head + 1) * HD]
    mixed_out[...] = stage[...].astype(bf16).reshape(KV, HEADS, HD)
    for peer in kv_peers:
        to_kv(6, mixed_out.at[peer], mixed_in.at[kv], peer).start()
    mixed_in[kv] = mixed_out[kv]
    all_kv(6, mixed_in).wait_recv()
    final = own_stream + jnp.sum(mixed_in[...].astype(f32), axis=0)
    for head in range(HEADS):
        out[:, head * HD : (head + 1) * HD] = final[head : head + 1].astype(bf16)

    all_kv(0, rotated).wait_send()
    all_kv(1, part_in).wait_send()
    near_kv(2, attended).wait_send()
    all_tp(3, square_in, TP - 1).wait_send()
    all_kv(6, mixed_out).wait_send()
    all_tp(5, hidden, 2).wait_send()
    all_tp(8, hidden, 4).wait_send()
    all_tp(9, hidden, 1).wait_send()

    @pl.when(tp < CHUNKS)
    def _():
        all_tp(4, sums_out, CHUNKS - 1).wait_send()

    @pl.when(tp == CHUNKS)
    def _():
        all_tp(4, sums_out, CHUNKS).wait_send()


def shards(
    queries,
    sign_bits,
    key_pages,
    value_pages,
    page_table,
    page_count,
    residual,
    norm_gain,
    gate_weight,
    up_weight,
    down_weight,
):
    in_hbm = pl.BlockSpec(memory_space=pltpu.HBM)
    result = pl.pallas_call(
        layer,
        out_shape=pltpu.VMEM((1, FEATURES), bf16),
        in_specs=[in_hbm] * 11,
        out_specs=pl.BlockSpec(memory_space=pltpu.VMEM),
        scratch_shapes=[
            pltpu.SMEM((1, SLOTS, KV), jnp.int32),
            pltpu.SMEM((1, KV), jnp.int32),
            pltpu.VMEM(queries.shape, bf16),
            pltpu.VMEM((1, HD), jnp.int32),
            pltpu.VMEM((1, 128), jnp.int32),
            pltpu.SMEM((1, 128), jnp.int32),
            pltpu.VMEM(key_pages.shape, bf16),
            pltpu.VMEM(value_pages.shape, bf16),
            pltpu.VMEM(residual.shape, bf16),
            pltpu.VMEM((FEATURES,), bf16),
            pltpu.VMEM((FEATURES, PADDED), bf16),
            pltpu.VMEM((FEATURES, PADDED), bf16),
            pltpu.VMEM((TP * CHUNK, FEATURES), bf16),
            pltpu.VMEM((KV, HEADS, HD), bf16),
            pltpu.VMEM((PAGES, HEADS, HD), f32),
            pltpu.VMEM((PAGES, HEADS, HD), f32),
            pltpu.VMEM((PAGES, HEADS, HD), f32),
            pltpu.VMEM((KV // 2, 3, HEADS, HD), bf16),
            pltpu.VMEM((KV, 3, HEADS, HD), bf16),
            pltpu.VMEM((KV // 2, 2, HEADS, HD), bf16),
            pltpu.VMEM((KV * HEADS, HD), f32),
            pltpu.VMEM((KV, FEATURES), bf16),
            pltpu.VMEM((KV, 128), bf16),
            pltpu.VMEM((TP, KV, 128), bf16),
            pltpu.VMEM((CHUNKS, KV, 2 * CHUNK), bf16),
            pltpu.VMEM((TP, KV, 2 * CHUNK), bf16),
            pltpu.VMEM((TP, KV, CHUNK), bf16),
            pltpu.VMEM((KV, FEATURES), f32),
            pltpu.VMEM((KV, HEADS, HD), bf16),
            pltpu.VMEM((KV, HEADS, HD), bf16),
            pltpu.SemaphoreType.DMA((12,)),
            pltpu.SemaphoreType.DMA((10,)),
            pltpu.SemaphoreType.DMA((10,)),
        ],
        compiler_params=pltpu.CompilerParams(
            collective_id=0, has_side_effects=True, vmem_limit_bytes=63 * 1024 * 1024
        ),
    )(
        jnp.transpose(page_table, (0, 2, 1)),
        page_count,
        queries,
        sign_bits.reshape(1, HD),
        key_pages,
        value_pages,
        residual,
        norm_gain,
        gate_weight,
        up_weight,
        down_weight,
    )
    return result


def solution(mesh):
    in_specs = (
        P("kv", "tp"),
        P(),
        P("kv", None, "tp"),
        P("kv", None, "tp"),
        P("kv", None, None),
        P("kv", None),
        P(None, "tp"),
        P("tp"),
        P("tp", "kv"),
        P("tp", "kv"),
        P("kv", "tp"),
    )
    out_specs = P("kv", "tp")
    return jax.shard_map(shards, mesh=mesh, in_specs=in_specs, out_specs=out_specs, check_vma=False)
```

```python
from functools import partial

import jax
import jax.numpy as jnp
from jax import lax
from jax.experimental import pallas as pl
from jax.experimental.pallas import tpu as pltpu
from jax.sharding import PartitionSpec as P

fill_value = -1e30
epsilon = 1e-05
f32 = jnp.float32
bf16 = jnp.bfloat16
MESH = pl.DeviceIdType.MESH

KV = 16
TP = 8
HEADS = 16
HD = 128
SLOTS = 4
PAGES = 32
FEATURES = HEADS * HD
UNITS = 1664
CHUNK = 256
CHUNKS = -(-UNITS // CHUNK)
PADDED = CHUNKS * CHUNK


def dot(left, right):
    return jnp.dot(left, right, preferred_element_type=f32)


def pair_of(kv):
    x, z = kv // 4, kv % 4
    return (x % 2) * 4 + (z + 2 * (x // 2)) % 4, x // 2


def split3(value):
    high = value.astype(bf16).astype(f32)
    rest = value - high
    middle = rest.astype(bf16).astype(f32)
    return high, middle, rest - middle


def in_lanes(parts):
    rows = parts[0].shape[0]
    lane = lax.broadcasted_iota(jnp.int32, (rows, 128), 1)
    tile = jnp.zeros((rows, 128), f32)
    for place, part in enumerate(parts):
        tile = jnp.where(lane == place, part, tile)
    return tile.astype(bf16)


def layer(
    table_hbm,
    count_hbm,
    queries_hbm,
    signs_hbm,
    keys_hbm,
    values_hbm,
    residual_hbm,
    gain_hbm,
    gate_hbm,
    up_hbm,
    down_hbm,
    out,
    table,
    count,
    queries,
    signs,
    owner_row,
    owner,
    keys,
    values,
    residual,
    gain,
    gate,
    up,
    down,
    rotated,
    page_max,
    page_total,
    page_out,
    part_out,
    part_in,
    attended,
    stage,
    scaled,
    sums_out,
    sums_in,
    hidden,
    product,
    mixed_out,
    mixed_in,
    load_sem,
    send_sem,
    recv_sem,
):
    kv = lax.axis_index("kv")
    tp = lax.axis_index("tp")

    loads = [
        pltpu.make_async_copy(source, target, load_sem.at[place])
        for place, (source, target) in enumerate(
            [
                (queries_hbm, queries),
                (signs_hbm, signs),
                (residual_hbm, residual),
                (gain_hbm, gain),
                (keys_hbm, keys),
                (values_hbm, values),
                (gate_hbm, gate.at[:, pl.ds(0, UNITS)]),
                (up_hbm, up.at[:, pl.ds(0, UNITS)]),
                (down_hbm, down.at[pl.ds(0, UNITS)]),
                (table_hbm, table),
                (count_hbm, count),
            ]
        )
    ]
    loads[0].start()
    loads[1].start()

    x, z = kv // 4, lax.rem(kv, 4)
    offsets = [(dx, dz) for dx in range(4) for dz in range(4) if dx or dz]
    offsets.sort(key=lambda at: -min(at[0], 4 - at[0]) - min(at[1], 4 - at[1]))
    kv_peers = [lax.rem(x + dx, 4) * 4 + lax.rem(z + dz, 4) for dx, dz in offsets]
    pair, member = pair_of(kv)
    near = [(0, 2), (1, 1), (3, 1), (0, 1), (0, 3), (1, 0), (3, 0)]
    near_peers = [lax.rem(x + dx, 4) * 4 + lax.rem(z + dz, 4) for dx, dz in near]

    y, core = tp // 2, tp % 2
    row = [
        lax.rem(y + dy, 4) * 2 + side
        for dy in (2, 3, 1, 0)
        for side in ((core, 1 - core) if dy else (1 - core, core))
    ]
    tp_peers = row[:-1]
    gap = sum(jnp.where(peer == TP - 1, place, 0) for place, peer in enumerate(row))
    chunk_order = [
        jnp.where(place < gap, row[place], row[place + 1]) for place in range(CHUNKS)
    ]

    barrier = pltpu.get_barrier_semaphore()
    for peer in kv_peers:
        pl.semaphore_signal(barrier, inc=1, device_id={"kv": peer}, device_id_type=MESH)
    for peer in tp_peers:
        pl.semaphore_signal(barrier, inc=1, device_id={"tp": peer}, device_id_type=MESH)

    for place in (9, 10, 2, 3, 4, 5, 6, 7, 8):
        loads[place].start()

    def to_kv(phase, source, target, peer):
        return pltpu.make_async_remote_copy(
            src_ref=source,
            dst_ref=target,
            send_sem=send_sem.at[phase],
            recv_sem=recv_sem.at[phase],
            device_id={"kv": peer},
            device_id_type=MESH,
        )

    def to_tp(phase, source, target, peer):
        return pltpu.make_async_remote_copy(
            src_ref=source,
            dst_ref=target,
            send_sem=send_sem.at[phase],
            recv_sem=recv_sem.at[phase],
            device_id={"tp": peer},
            device_id_type=MESH,
        )

    def all_kv(phase, buffer):
        return to_kv(phase, buffer.at[pl.ds(0, KV - 1)], buffer.at[pl.ds(0, KV - 1)], kv)

    row = lax.broadcasted_iota(jnp.int32, (HD, HD), 0)
    column = lax.broadcasted_iota(jnp.int32, (HD, HD), 1)
    common = row & column
    parity = common
    for shift in (4, 2, 1):
        parity = parity ^ (parity >> shift)
    turn = ((1 - 2 * (parity & 1)).astype(f32) * (1.0 / HD)).astype(bf16)
    loads[0].wait()
    loads[1].wait()
    wide = queries[...].astype(f32)
    heads = jnp.concatenate(
        [wide[:, head * HD : (head + 1) * HD] for head in range(HEADS)], axis=0
    )
    sign = (1 - 2 * signs[...]).astype(f32)
    rotated[kv] = dot((heads * sign).astype(bf16), turn).astype(bf16)

    pl.semaphore_wait(barrier, KV + TP - 2)

    for peer in kv_peers:
        to_kv(0, rotated.at[kv], rotated.at[kv], peer).start()

    loads[9].wait()
    loads[10].wait()
    page_lane = lax.broadcasted_iota(jnp.int32, (1, 128), 1)
    owners = jnp.zeros((1, 128), jnp.int32)
    for request in range(KV):
        for slot in range(SLOTS):
            page = jnp.where(slot < count[0, request], table[0, slot, request], -1)
            owners = jnp.where(page_lane == page, request, owners)
    owner_row[...] = owners
    owner_copy = pltpu.make_async_copy(owner_row, owner, load_sem.at[11])
    owner_copy.start()
    gate[:, UNITS:] = jnp.zeros((FEATURES, PADDED - UNITS), bf16)
    up[:, UNITS:] = jnp.zeros((FEATURES, PADDED - UNITS), bf16)
    down[UNITS:, :] = jnp.zeros((TP * CHUNK - UNITS, FEATURES), bf16)

    loads[2].wait()
    loads[3].wait()
    for head in range(HEADS):
        stage[pl.ds(head, KV, stride=HEADS), :] = residual[:, head * HD : (head + 1) * HD].astype(
            f32
        )
    own_residual = stage[pl.ds(pl.multiple_of(kv * HEADS, HEADS), HEADS), :]

    owner_copy.wait()
    loads[4].wait()
    loads[5].wait()
    all_kv(0, rotated).wait_recv()

    pages = range(PAGES)
    scores = [
        lax.dot_general(
            rotated[owner[0, page]],
            keys[page],
            (((1,), (1,)), ((), ())),
            preferred_element_type=f32,
        )
        for page in pages
    ]
    largest = [jnp.max(score, axis=1, keepdims=True) for score in scores]
    weights = [jnp.exp(score - best).astype(bf16) for score, best in zip(scores, largest)]
    totals = [jnp.sum(weight.astype(f32), axis=1, keepdims=True) for weight in weights]
    for page in pages:
        page_max[page] = jnp.broadcast_to(largest[page], (HEADS, HD))
        page_total[page] = jnp.broadcast_to(totals[page], (HEADS, HD))

    lane = lax.broadcasted_iota(jnp.int32, (HEADS, 128), 1)
    levels = jnp.zeros((HEADS, 128), f32)
    owned = [[table[0, slot, request] for slot in range(SLOTS)] for request in range(KV)]
    shares = []
    for request in range(KV):
        live = count[0, request]
        tops = [
            jnp.where(slot < live, page_max[page], fill_value)
            for slot, page in enumerate(owned[request])
        ]
        best = jnp.maximum(jnp.maximum(tops[0], tops[1]), jnp.maximum(tops[2], tops[3]))
        factors = [jnp.exp(top - best) for top in tops]
        total = sum(factor * page_total[page] for factor, page in zip(factors, owned[request]))
        inverse_total = 1.0 / total
        shares.append([factor * inverse_total for factor in factors])
        which, place = pair_of(request)
        for part, value in enumerate(split3(best + jnp.log(total))):
            levels = jnp.where(lane == part * KV + 2 * which + place, value, levels)
    level_tile = levels.astype(bf16)
    for which in range(KV // 2):
        part_out[which, 2] = level_tile
    outs = [dot(weight, values[page]) for page, weight in zip(pages, weights)]
    for page in pages:
        page_out[page] = outs[page]
    merged = [
        sum(share * page_out[page] for share, page in zip(shares[request], owned[request]))
        for request in range(KV)
    ]
    for request in range(KV):
        which, place = pair_of(request)
        part_out[which, place] = merged[request].astype(bf16)
    for peer in kv_peers:
        to_kv(1, part_out.at[pair_of(peer)[0]], part_in.at[kv], peer).start()
    part_in[kv] = part_out[pair]

    picked_lane = lax.broadcasted_iota(jnp.int32, (128, 2 * HD), 0)
    picked_column = lax.broadcasted_iota(jnp.int32, (128, 2 * HD), 1)
    pick = (
        (picked_lane < 3 * KV)
        & (lax.rem(picked_lane, KV) == 2 * pair + jnp.where(picked_column < HD, 0, 1))
    ).astype(f32).astype(bf16)
    all_kv(1, part_in).wait_recv()
    level = dot(part_in[:, 2].reshape(KV * HEADS, 128), pick).reshape(KV, HEADS, 2 * HD)
    factor = jnp.exp(level - jnp.max(level, axis=0, keepdims=True))
    whole = jnp.sum(factor, axis=0)
    inverse_whole = 1.0 / whole
    both = [
        jnp.sum(factor[:, :, place * HD : (place + 1) * HD] * part_in[:, place].astype(f32), axis=0)
        * inverse_whole[:, place * HD : (place + 1) * HD]
        for place in range(2)
    ]
    for place in range(2):
        attended[pair, place] = both[place].astype(bf16)
    for peer in near_peers:
        to_kv(2, attended.at[pair], attended.at[pair], peer).start()
    attention = jnp.where(member == 0, both[0], both[1]).astype(bf16)
    own_stream = own_residual + attention.astype(f32)

    def near_kv(phase, buffer):
        return to_kv(phase, buffer.at[pl.ds(0, 7)], buffer.at[pl.ds(0, 7)], kv)

    near_kv(2, attended).wait_recv()
    for request in range(KV):
        which, place = pair_of(request)
        stage[request * HEADS : (request + 1) * HEADS, :] = attended[which, place].astype(f32)
    squares = jnp.zeros((KV, HD), f32)
    for head in range(HEADS):
        span = slice(head * HD, (head + 1) * HD)
        piece = residual[:, span].astype(f32) + stage[pl.ds(head, KV, stride=HEADS), :]
        squares = squares + piece * piece
        scaled[:, span] = (piece * gain[span].astype(f32)[None, :]).astype(bf16)
    square_tile = in_lanes(split3(jnp.sum(squares, axis=1, keepdims=True)))

    loads[6].wait()
    loads[7].wait()

    for step, peer in enumerate(chunk_order):
        span = pl.ds(pl.multiple_of(peer * CHUNK, CHUNK), CHUNK)
        sums_out[peer, :, :CHUNK] = dot(scaled[...], gate[:, span]).astype(bf16)
        sums_out[peer, :, CHUNK : 2 * CHUNK] = dot(scaled[...], up[:, span]).astype(bf16)
        sums_out[peer, :, 2 * CHUNK :] = square_tile
        if step < CHUNKS - 1:
            to_tp(4, sums_out.at[peer], sums_in.at[tp], peer).start()

    @pl.when(tp == CHUNKS)
    def _():
        to_tp(4, sums_out.at[CHUNKS - 1], sums_in.at[tp], CHUNKS - 1).start()

    def all_tp(phase, buffer, size):
        return to_tp(phase, buffer.at[pl.ds(0, size)], buffer.at[pl.ds(0, size)], tp)

    @pl.when(tp < CHUNKS)
    def _():
        sums_in[tp] = sums_out[tp]
        all_tp(4, sums_in, TP - 1).wait_recv()
        total = jnp.sum(sums_in[...].astype(f32), axis=0)
        mean = jnp.sum(total[:, 2 * CHUNK :], axis=1, keepdims=True) / (FEATURES * TP)
        inverse = lax.rsqrt(mean + epsilon)
        value = total[:, :CHUNK] * inverse
        hidden[tp] = (
            value / (1.0 + jnp.exp(-value)) * (total[:, CHUNK : 2 * CHUNK] * inverse)
        ).astype(bf16)

    @pl.when(tp == CHUNKS)
    def _():
        hidden[CHUNKS] = jnp.zeros((KV, CHUNK), bf16)

    for peer in tp_peers[:2]:
        to_tp(5, hidden.at[tp], hidden.at[tp], peer).start()
    for peer in tp_peers[2:6]:
        to_tp(8, hidden.at[tp], hidden.at[tp], peer).start()
    sibling = tp_peers[6]
    to_tp(9, hidden.at[tp], hidden.at[tp], sibling).start()

    def chip_product(chip):
        units = jnp.concatenate([hidden[2 * chip], hidden[2 * chip + 1]], axis=1)
        return dot(units, down[pl.ds(pl.multiple_of(chip * 2 * CHUNK, 2 * CHUNK), 2 * CHUNK), :])

    loads[8].wait()
    to_tp(9, hidden.at[sibling], hidden.at[sibling], sibling).wait_recv()
    product[...] = chip_product(y)
    all_tp(8, hidden, 4).wait_recv()
    product[...] += chip_product(lax.rem(y + 1, 4)) + chip_product(lax.rem(y + 3, 4))
    all_tp(5, hidden, 2).wait_recv()
    result = product[...] + chip_product(lax.rem(y + 2, 4))
    for head in range(HEADS):
        stage[pl.ds(head, KV, stride=HEADS), :] = result[:, head * HD : (head + 1) * HD]
    mixed_out[...] = stage[...].astype(bf16).reshape(KV, HEADS, HD)
    for peer in kv_peers:
        to_kv(6, mixed_out.at[peer], mixed_in.at[kv], peer).start()
    mixed_in[kv] = mixed_out[kv]
    all_kv(6, mixed_in).wait_recv()
    final = own_stream + jnp.sum(mixed_in[...].astype(f32), axis=0)
    for head in range(HEADS):
        out[:, head * HD : (head + 1) * HD] = final[head : head + 1].astype(bf16)

    all_kv(0, rotated).wait_send()
    all_kv(1, part_in).wait_send()
    near_kv(2, attended).wait_send()
    all_kv(6, mixed_out).wait_send()
    all_tp(5, hidden, 2).wait_send()
    all_tp(8, hidden, 4).wait_send()
    all_tp(9, hidden, 1).wait_send()

    @pl.when(tp < CHUNKS)
    def _():
        all_tp(4, sums_out, CHUNKS - 1).wait_send()

    @pl.when(tp == CHUNKS)
    def _():
        all_tp(4, sums_out, CHUNKS).wait_send()


def shards(
    queries,
    sign_bits,
    key_pages,
    value_pages,
    page_table,
    page_count,
    residual,
    norm_gain,
    gate_weight,
    up_weight,
    down_weight,
):
    in_hbm = pl.BlockSpec(memory_space=pltpu.HBM)
    result = pl.pallas_call(
        layer,
        out_shape=pltpu.VMEM((1, FEATURES), bf16),
        in_specs=[in_hbm] * 11,
        out_specs=pl.BlockSpec(memory_space=pltpu.VMEM),
        scratch_shapes=[
            pltpu.SMEM((1, SLOTS, KV), jnp.int32),
            pltpu.SMEM((1, KV), jnp.int32),
            pltpu.VMEM(queries.shape, bf16),
            pltpu.VMEM((1, HD), jnp.int32),
            pltpu.VMEM((1, 128), jnp.int32),
            pltpu.SMEM((1, 128), jnp.int32),
            pltpu.VMEM(key_pages.shape, bf16),
            pltpu.VMEM(value_pages.shape, bf16),
            pltpu.VMEM(residual.shape, bf16),
            pltpu.VMEM((FEATURES,), bf16),
            pltpu.VMEM((FEATURES, PADDED), bf16),
            pltpu.VMEM((FEATURES, PADDED), bf16),
            pltpu.VMEM((TP * CHUNK, FEATURES), bf16),
            pltpu.VMEM((KV, HEADS, HD), bf16),
            pltpu.VMEM((PAGES, HEADS, HD), f32),
            pltpu.VMEM((PAGES, HEADS, HD), f32),
            pltpu.VMEM((PAGES, HEADS, HD), f32),
            pltpu.VMEM((KV // 2, 3, HEADS, HD), bf16),
            pltpu.VMEM((KV, 3, HEADS, HD), bf16),
            pltpu.VMEM((KV // 2, 2, HEADS, HD), bf16),
            pltpu.VMEM((KV * HEADS, HD), f32),
            pltpu.VMEM((KV, FEATURES), bf16),
            pltpu.VMEM((CHUNKS, KV, 2 * CHUNK + 128), bf16),
            pltpu.VMEM((TP, KV, 2 * CHUNK + 128), bf16),
            pltpu.VMEM((TP, KV, CHUNK), bf16),
            pltpu.VMEM((KV, FEATURES), f32),
            pltpu.VMEM((KV, HEADS, HD), bf16),
            pltpu.VMEM((KV, HEADS, HD), bf16),
            pltpu.SemaphoreType.DMA((12,)),
            pltpu.SemaphoreType.DMA((10,)),
            pltpu.SemaphoreType.DMA((10,)),
        ],
        compiler_params=pltpu.CompilerParams(
            collective_id=0, has_side_effects=True, vmem_limit_bytes=63 * 1024 * 1024
        ),
    )(
        jnp.transpose(page_table, (0, 2, 1)),
        page_count,
        queries,
        sign_bits.reshape(1, HD),
        key_pages,
        value_pages,
        residual,
        norm_gain,
        gate_weight,
        up_weight,
        down_weight,
    )
    return result


def solution(mesh):
    in_specs = (
        P("kv", "tp"),
        P(),
        P("kv", None, "tp"),
        P("kv", None, "tp"),
        P("kv", None, None),
        P("kv", None),
        P(None, "tp"),
        P("tp"),
        P("tp", "kv"),
        P("tp", "kv"),
        P("kv", "tp"),
    )
    out_specs = P("kv", "tp")
    return jax.shard_map(shards, mesh=mesh, in_specs=in_specs, out_specs=out_specs, check_vma=False)
```
